256 devices in a mesh: section: 64 (over z, y_lo, x), head: 4 (over y_hi, core).
Axes of the slice: x: 4, y: 4 (y_hi: 2, y_lo: 2; y = y_hi * 2 + y_lo), z: 8, core: 2. Of those that a mesh axis runs over, the one named last changes fastest.
Arguments:
- entering_hidden: bfloat16 [64, 128, 1792], P('section', None, 'head'), may hold values from -6 to 6
- entering_embed: bfloat16 [64, 128, 1792], P('section', None, 'head'), may hold values from -6 to 6
- incoming_embed: bfloat16 [1, 128, 1792], P(None, None, 'head'), may hold values from -6 to 6
- mixer_input_weight: bfloat16 [64, 1792, 3584], P('section', None, 'head'), may hold values from -0.125 to 0.125
- input_output_matrix_weight: bfloat16 [64, 1792, 128], P('section'), may hold values from -0.125 to 0.125
- step_size_weight: bfloat16 [64, 1792, 56], P('section', None, 'head'), may hold values from -0.125 to 0.125
- mixer_output_weight: bfloat16 [64, 3584, 1792], P('section', 'head'), may hold values from -0.09375 to 0.09375
- log_decay_rate: float32 [64, 56], P('section', 'head'), may hold values from -5 to 0
- step_size_bias: float32 [64, 56], P('section', 'head'), may hold values from -4 to -1
- skip_weight: float32 [64, 56], P('section', 'head'), may hold values from 0.5 to 1.5
- shared_query_key_value: bfloat16 [3584, 3, 3584], P('section', None, 'head'), may hold values from -6 to 6
- shared_output_weight: bfloat16 [1792, 3584], P('section', 'head'), may hold values from -0.09375 to 0.09375
- adapter_down: bfloat16 [64, 3584, 128], P('section'), may hold values from -0.09375 to 0.09375
- adapter_upward: bfloat16 [64, 128, 3, 3584], P('section', None, None, 'head'), may hold values from -0.5 to 0.5
- calls: int32 [64], P('section'), may hold values from 0 to 1, as said below
Outputs:
- section_outputs: bfloat16 [2, 64, 128, 1792], P(None, 'section', None, 'head')
The draws below stay inside these ranges and needn't reach their ends.
Inputs may be any that keep to these rules, and one draw needn't show every extreme that they name: `calls`: the calling sections are every third section, starting at one of sections 0, 1 and 2; all others hold 0.
All inputs are finite; a program needn't handle non-finite values.
Results may differ from the reference program's by a relative error of at most 0.018.
Values may be sent and summed in bfloat16 or wider, within the bound.
A program may use at most 128 MiB of HBM per device.

```python
import jax
import jax.numpy as jnp
from jax import lax

D = 1792
NH = 56
P_SIZE = 64
N = 64
HALF_HEADS = 16
HEAD_WIDTH = 224
ADAPTER_RANK = 128
SEQ = 128
ROUNDS = 2
RELAY_SECTIONS = 64
JOINED_FEATURES = 3584


def draw_calls(key, part):
    key = jax.random.fold_in(key, 11)
    offset = jax.random.randint(key, (), 0, 3)
    sections = jnp.arange(RELAY_SECTIONS)
    return ((sections + offset) % 3 == 0).astype(jnp.int32)


def draw_shared_query_key_value(key, part):
    key = jax.random.fold_in(key, 23)
    base = jax.random.truncated_normal(key, -4.0, 4.0, (JOINED_FEATURES, 3, HALF_HEADS * HEAD_WIDTH), jnp.float32) * JOINED_FEATURES ** (-0.5)
    return base.astype(jnp.bfloat16)


def level_of(key, extent, pieces, smallest, top_value):
    loudness = 1.0
    for axis_at, parts in pieces:
        steps = jax.random.uniform(jax.random.fold_in(jax.random.fold_in(key, 6), axis_at), (parts,), jnp.float32, smallest / len(pieces), top_value / len(pieces))
        loudness = loudness * jnp.repeat(jnp.exp(steps), extent[axis_at] // parts).reshape((-1,) + (1,) * (len(extent) - 1 - axis_at))
    return loudness


def gaussian(key, shape, spread, most, shards=(), held_as=jnp.bfloat16):
    drawn = spread * jax.random.normal(key, shape, jnp.float32)
    if shards:
        drawn = drawn * level_of(key, shape, shards, -0.22, 0.18)
    return jnp.clip(drawn, -most, most).astype(held_as)


def setup_inputs(seed: int = 0) -> dict:
    key_of = jax.random.split(jax.random.key(seed), 16)
    entering_hidden = gaussian(key_of[0], (RELAY_SECTIONS, SEQ, D), 1.0, 6.0, ((0, 64), (2, 4)))
    entering_embed = gaussian(key_of[1], (RELAY_SECTIONS, SEQ, D), 1.0, 6.0, ((0, 64), (2, 4)))
    incoming_embed = gaussian(key_of[2], (ROUNDS - 1, SEQ, D), 1.0, 6.0, ((2, 4),))
    mixer_input_weight = gaussian(key_of[3], (RELAY_SECTIONS, D, NH * P_SIZE), D ** -0.5, 0.125, ((0, 64), (2, 4)))
    input_output_matrix_weight = gaussian(key_of[4], (RELAY_SECTIONS, D, 2 * N), D ** -0.5, 0.125, ((0, 64),))
    step_size_weight = gaussian(key_of[5], (RELAY_SECTIONS, D, NH), D ** -0.5, 0.125, ((0, 64), (2, 4)))
    mixer_output_weight = gaussian(key_of[6], (RELAY_SECTIONS, NH * P_SIZE, D), (NH * P_SIZE) ** -0.5, 0.09375, ((0, 64), (1, 4)))
    log_decay_rate = jnp.clip(-5.0 + 5.0 * jax.random.uniform(key_of[7], (RELAY_SECTIONS, NH), jnp.float32) ** level_of(key_of[7], (RELAY_SECTIONS, NH), ((0, 64), (1, 4)), -0.2, 0.2), -5.0, 0.0)
    step_size_bias = jnp.clip(-4.0 + 3.0 * jax.random.uniform(key_of[8], (RELAY_SECTIONS, NH), jnp.float32) ** level_of(key_of[8], (RELAY_SECTIONS, NH), ((0, 64), (1, 4)), -0.2, 0.2), -4.0, -1.0)
    skip_weight = jnp.clip(0.5 + 1.0 * jax.random.uniform(key_of[9], (RELAY_SECTIONS, NH), jnp.float32) ** level_of(key_of[9], (RELAY_SECTIONS, NH), ((0, 64), (1, 4)), -0.2, 0.2), 0.5, 1.5)
    shared_query_key_value = draw_shared_query_key_value(jax.random.fold_in(key_of[15], 71), 0)
    shared_output_weight = gaussian(key_of[11], (D, HALF_HEADS * HEAD_WIDTH), (HALF_HEADS * HEAD_WIDTH) ** -0.5, 0.09375, ((0, 64), (1, 4)))
    adapter_down = gaussian(key_of[12], (RELAY_SECTIONS, JOINED_FEATURES, ADAPTER_RANK), JOINED_FEATURES ** -0.5, 0.09375, ((0, 64),))
    adapter_upward = gaussian(key_of[13], (RELAY_SECTIONS, ADAPTER_RANK, 3, HALF_HEADS * HEAD_WIDTH), ADAPTER_RANK ** -0.5, 0.5, ((0, 64), (3, 4)))
    calls = draw_calls(jax.random.fold_in(key_of[15], 71), 0)
    return dict(entering_hidden=entering_hidden, entering_embed=entering_embed, incoming_embed=incoming_embed, mixer_input_weight=mixer_input_weight, input_output_matrix_weight=input_output_matrix_weight, step_size_weight=step_size_weight, mixer_output_weight=mixer_output_weight, log_decay_rate=log_decay_rate, step_size_bias=step_size_bias, skip_weight=skip_weight, shared_query_key_value=shared_query_key_value, shared_output_weight=shared_output_weight, adapter_down=adapter_down, adapter_upward=adapter_upward, calls=calls)


def normed(values):
    return values * lax.rsqrt(lax.optimization_barrier(jnp.mean(values * values, axis=-1, keepdims=True)) + 1e-05)

def attend(query, keys, values):
    length = query.shape[0]
    heads = query.shape[1] // HEAD_WIDTH
    query = query.reshape(length, heads, HEAD_WIDTH).astype(jnp.float32)
    keys = keys.reshape(length, heads, HEAD_WIDTH).astype(jnp.float32)
    values = values.reshape(length, heads, HEAD_WIDTH).astype(jnp.float32)
    scores = jnp.einsum('qhd,khd->hqk', query, keys) * HEAD_WIDTH ** (-0.5)
    causal = jnp.arange(length)[:, None] >= jnp.arange(length)[None, :]
    scores = jnp.where(causal[None], scores, -1e+30)
    top = lax.optimization_barrier(jnp.max(scores, axis=-1, keepdims=True))
    expd = jnp.exp(scores - top)
    probs = (expd / lax.optimization_barrier(jnp.sum(expd, axis=-1, keepdims=True))).astype(jnp.bfloat16)
    mixed = jnp.einsum('hqk,khd->qhd', probs.astype(jnp.float32), values)
    return mixed.reshape(length, heads * HEAD_WIDTH).astype(jnp.bfloat16)

def scan_mix(inputs, bmat, cmat, steps, log_decay_rate, skip_weight):
    length = inputs.shape[0]
    heads = steps.shape[1]
    rate = steps * jnp.exp(log_decay_rate)[None, :]
    total = jnp.cumsum(rate, axis=0).T
    causal = jnp.arange(length)[:, None] >= jnp.arange(length)[None, :]
    gap = jnp.where(causal[None], total[:, :, None] - total[:, None, :], 0.0)
    decay = jnp.where(causal[None], jnp.exp(-gap), 0.0)
    inner = jnp.dot(cmat, bmat.T, precision=lax.Precision.HIGHEST)
    mixing = inner[None] * decay * steps.T[:, None, :]
    split_in = inputs.reshape(length, heads, P_SIZE)
    out = jnp.einsum('htj,jhp->thp', mixing, split_in, precision=lax.Precision.HIGHEST)
    out = out + skip_weight[None, :, None] * split_in
    return out.reshape(length, heads * P_SIZE).astype(jnp.bfloat16)

def advance_section(hidden_rows, embed_rows, mixer_input_weight, input_output_matrix_weight, step_size_weight, mixer_output_weight, log_decay_rate, step_size_bias, skip_weight, adapter_down, adapter_upward, marker_value, shared_query_key_value, shared_output_weight):
    joined = jnp.concatenate([hidden_rows, embed_rows], axis=1).astype(jnp.float32)
    gate_values = normed(joined).astype(jnp.bfloat16)
    projected_rows = jnp.dot(gate_values, shared_query_key_value.reshape(JOINED_FEATURES, 3 * HALF_HEADS * HEAD_WIDTH), preferred_element_type=jnp.float32)
    lowrank_update = jnp.dot(gate_values, adapter_down, preferred_element_type=jnp.float32).astype(jnp.bfloat16)
    projected_rows = projected_rows + jnp.dot(lowrank_update, adapter_upward.reshape(ADAPTER_RANK, 3 * HALF_HEADS * HEAD_WIDTH), preferred_element_type=jnp.float32)
    projected_rows = projected_rows.reshape(SEQ, 3, HALF_HEADS * HEAD_WIDTH).astype(jnp.bfloat16)
    mixed = attend(projected_rows[:, 0], projected_rows[:, 1], projected_rows[:, 2])
    attn = lax.dot_general(mixed, shared_output_weight, (((1,), (1,)), ((), ())), preferred_element_type=jnp.float32)
    middle = (hidden_rows.astype(jnp.float32) + marker_value.astype(jnp.float32) * attn).astype(jnp.bfloat16)
    unit = normed(middle.astype(jnp.float32)).astype(jnp.bfloat16)
    inputs = jax.nn.silu(jnp.dot(unit, mixer_input_weight, preferred_element_type=jnp.float32))
    states = jax.nn.silu(jnp.dot(unit, input_output_matrix_weight, preferred_element_type=jnp.float32))
    steps = jax.nn.softplus(jnp.dot(unit, step_size_weight, preferred_element_type=jnp.float32) + step_size_bias[None, :])
    mixed_ssm = scan_mix(inputs, states[:, :N], states[:, N:], steps, log_decay_rate, skip_weight)
    out = jnp.dot(mixed_ssm, mixer_output_weight, preferred_element_type=jnp.float32)
    return (middle.astype(jnp.float32) + out).astype(jnp.bfloat16)

def reference(entering_hidden, entering_embed, incoming_embed, mixer_input_weight, input_output_matrix_weight, step_size_weight, mixer_output_weight, log_decay_rate, step_size_bias, skip_weight, shared_query_key_value, shared_output_weight, adapter_down, adapter_upward, calls):
    relay_step_function = jax.vmap(advance_section, in_axes=(0, 0, 0, 0, 0, 0, 0, 0, 0, 0, 0, 0, None, None))
    hidden_rows = entering_hidden
    embed_rows = entering_embed
    results = []
    for rnd in range(ROUNDS):
        if rnd > 0:
            fresh = incoming_embed[rnd - 1][None]
            hidden_rows = jnp.concatenate([fresh, results[-1][:-1]], axis=0)
            embed_rows = jnp.concatenate([fresh, embed_rows[:-1]], axis=0)
        step_result = relay_step_function(hidden_rows, embed_rows, mixer_input_weight, input_output_matrix_weight, step_size_weight, mixer_output_weight, log_decay_rate, step_size_bias, skip_weight, adapter_down, adapter_upward, calls, shared_query_key_value, shared_output_weight)
        results.append(step_result)
    return jnp.stack(results, axis=0)
```

```python
import jax
import jax.numpy as jnp
from jax import lax
from jax.experimental import pallas as pl
from jax.experimental.pallas import tpu as pltpu
from jax.sharding import PartitionSpec as P

MESH = pl.DeviceIdType.MESH
BF = jnp.bfloat16
F32 = jnp.float32
NT = (((1,), (1,)), ((), ()))
TN = (((0,), (0,)), ((), ()))
HIGH = lax.Precision.HIGHEST
D = 1792
Q = 448
SEQ = 128
HEADS = 14
HEAD_WIDTH = 224
EPS = 1e-05
SENDS = 128


def iota(shape, dim):
    return lax.broadcasted_iota(jnp.int32, shape, dim)


def dot(a, b, dims=(((1,), (0,)), ((), ()))):
    return lax.dot_general(a, b, dims, preferred_element_type=F32)


def silu(v):
    return v / (1.0 + jnp.exp(-v))


def softplus(v):
    return jnp.maximum(v, 0.0) + jnp.log(1.0 + jnp.exp(-jnp.abs(v)))


def kernel(
    h0_in, e0_in, inc_in, wmix_in, wio_in, wdt_ref, wom_in, decay_ref, bias_ref, skip_ref,
    qkv_in, wo_ref, down_in, up_in, calls_ref,
    out_ref,
    xall, xs, wg, wmix, wio, wom, down, up, qw, sel, a2s, a2r, wo32, ups, upr, low, misc,
    acc, wog, mx, rs2s, rs2r, atb, atr, mid, hf, mbuf, ubuf, ybuf, xbuf, pbuf, cbuf, rss, rsr,
    outq, send_sem, recv_sem, load_sem,
):
    s = lax.axis_index("section")
    h = lax.axis_index("head")
    x = lax.rem(s, 4)
    y = lax.rem(s // 4, 2)
    z = s // 8
    core = lax.rem(h, 2)
    base = s - x
    sec_up = lax.rem(z + 1, 8) * 8 + lax.rem(s, 8)
    sec_down = lax.rem(z + 7, 8) * 8 + lax.rem(s, 8)
    sec_y = s + 4 - 8 * y
    sec_next = lax.rem(s + 1, 64)
    sec_prev = lax.rem(s + 63, 64)
    x_next = lax.rem(x + 1, 4)

    def line(j):
        return lax.rem(x + j, 4)

    def sib(j):
        return lax.rem(h + j, 4)

    index = {}
    descs = {}

    def remote(key, src, dst, section, head):
        at = index.setdefault(key, len(index))
        desc = pltpu.make_async_remote_copy(
            src_ref=src, dst_ref=dst, send_sem=send_sem.at[at], recv_sem=recv_sem.at[at],
            device_id={"section": section, "head": head}, device_id_type=MESH,
        )
        descs[key] = desc
        return desc

    def start(key, src, dst, section=None, head=None):
        remote(key, src, dst, s if section is None else section, h if head is None else head).start()

    def pass_on(key, src, dst):
        fresh = remote((key,), inc_in, dst, sec_next, h)
        usual = remote((key,), src, dst, sec_next, h)
        pl.when(s == 63)(lambda: fresh.start())
        pl.when(s != 63)(lambda: usual.start())

    def got(*key):
        descs[key].wait_recv()

    loads = {}

    def load(name, src, dst):
        loads[name] = pltpu.make_async_copy(src, dst, load_sem.at[len(loads)])
        loads[name].start()

    own = pl.ds(pl.multiple_of(h * Q, Q), Q)
    load("qkv", qkv_in, qw)
    load("h0", h0_in, xall.at[x, 0, own])
    load("e0", e0_in, xall.at[x, 1, own])
    load("down", down_in, down)
    load("up", up_in, up)
    load("wmix", wmix_in, wmix)
    load("wio", wio_in, wio)
    load("wom", wom_in, wom)

    barrier = pltpu.get_barrier_semaphore()
    peers = [(base + line(j), h) for j in (1, 2, 3)] + [(s, sib(j)) for j in (1, 2, 3)]
    peers += [(sec_up, h), (sec_down, h), (sec_y, h), (sec_next, h), (sec_prev, h)]
    for section, head in peers:
        pl.semaphore_signal(
            barrier, inc=1, device_id={"section": section, "head": head}, device_id_type=MESH
        )
    for i in range(4):
        r, c = iota((896, 256), 0), iota((896, 256), 1)
        sel[i] = jnp.where((r == c + 224 * i) & (c < 224), 1.0, 0.0).astype(BF)
    wo32[...] = jnp.zeros_like(wo32)
    wo32[0:28, :] = wo_ref[...]
    pl.semaphore_wait(barrier, len(peers))

    def gather_heads(name, src, dst_of):
        for j in (1, 2, 3):
            start((name, j), src, dst_of, None, sib(j))

    def wait_heads(name):
        for j in (1, 2, 3):
            got(name, j)

    gather_heads("h0", h0_in, xall.at[x, 0, own])
    gather_heads("e0", e0_in, xall.at[x, 1, own])

    pass_on("e1p", e0_in, xall.at[x_next, 3, own])

    loads["qkv"].wait()
    for i in range(4):
        for k in range(3):
            block = dot(qw[k], sel[i])
            block = jnp.concatenate([block, jnp.zeros((8, 256), F32)], axis=0)
            a2s[i, :, 256 * k : 256 * k + 256] = block.astype(BF)
    for j in (1, 2, 3):
        start(("a2a", j), a2s.at[line(j)], a2r.at[x], base + line(j))
    a2r[x] = a2s[x]
    for i in range(3):
        wg[z, y, 224:256, 256 * i : 256 * i + 256] = dot(wo32[...], sel[i]).astype(BF)
    last = dot(wo32[...], sel[3]).astype(BF)
    wg[z, y, 256:272, 0:256] = last[0:16]
    wg[z, y, 256:272, 256:512] = last[16:32]
    wg[z, y, 256:272, 512:768] = jnp.zeros((16, 256), BF)
    r, c = iota((224, 256), 0), iota((224, 256), 1)
    compact = jnp.where(((c - 8 * (c >> 6)) == r) & ((c & 63) < 56), 1.0, 0.0).astype(BF)
    for j in (1, 2, 3):
        got("a2a", j)
    packed = jnp.concatenate([a2r[0], a2r[1], a2r[2], a2r[3]], axis=0)
    wg[z, y, 0:224, :] = dot(compact, packed).astype(BF)

    halves = {None: (0, 272), 0: (0, 144), 1: (144, 128)}

    def piece(other, dz, half):
        first, rows = halves[half]
        return wg.at[lax.rem(z + dz + 8, 8), (1 - y) if other else y, pl.ds(first, rows)]

    def push(way, other, dz, half=None):
        ref = piece(other, dz, half)
        section = {"down": sec_down, "up": sec_up, "y": sec_y}[way]
        start((way, other, dz, half), ref, ref, section)

    def pump(step):
        if step == 0:
            push("down", 0, 0)
            push("up", 0, 0)
            push("y", 0, 0)
        if step == 1:
            got("down", 0, 0, None)
            push("down", 0, 1)
            push("y", 0, 1)
            got("up", 0, 0, None)
            push("up", 0, -1)
        if step == 2:
            got("down", 0, 1, None)
            push("down", 0, 2)
            push("y", 0, 2)
            got("up", 0, -1, None)
            push("up", 0, -2)
            push("y", 0, -2)
        if step == 3:
            got("down", 0, 2, None)
            push("down", 0, 3, 0)
            got("up", 0, -2, None)
            push("up", 0, -3, 1)
            push("y", 0, -1)
        if step == 4:
            got("y", 0, 0, None)
            got("y", 0, 1, None)
            got("y", 0, 2, None)
            push("down", 1, 2)
            got("y", 0, -2, None)
            push("up", 1, -2)
        if step == 5:
            got("down", 1, 2, None)
            push("down", 1, 3, 0)
            got("up", 1, -2, None)
            push("up", 1, -3, 1)
        if step == 6:
            got("y", 0, -1, None)
            got("down", 0, 3, 0)
            got("up", 0, -3, 1)
            got("down", 1, 3, 0)
            got("up", 1, -3, 1)

    pump(0)

    half_rows = pl.ds(pl.multiple_of(core * 896, 896), 896)
    twin = h + 1 - 2 * core

    def gather_line(n):
        for j in (1, 2, 3):
            ref = xall.at[x, n, half_rows]
            start(("line", n, j), ref, ref, base + line(j))

    def share_line(n):
        for j in (1, 2, 3):
            got("line", n, j)
            ref = xall.at[line(4 - j), n, half_rows]
            start(("twin", n, j), ref, ref, None, twin)

    def wait_share(n):
        for j in (1, 2, 3):
            got("twin", n, j)

    def row_scale(n):
        total = jnp.zeros((1, SEQ), F32)
        for part in (0, 1):
            def add(t, total):
                block = xall[x, 2 * n + part, pl.ds(pl.multiple_of(t * 128, 128), 128), :].astype(F32)
                return total + jnp.sum(block * block, axis=0, keepdims=True)
            total = lax.fori_loop(0, 14, add, total)
        return lax.rsqrt(total / (2 * D) + EPS)

    def make_low(n):
        scale = row_scale(n)
        total = jnp.zeros((128, SEQ), F32)
        for part in (0, 1):
            total = total + dot(down[part * D : part * D + D, :], xall[x, 2 * n + part], TN)
        low[x, n] = (total * scale).astype(BF)
        rows = iota((8, 128), 0)
        mark = calls_ref[0].astype(F32)
        misc[x, n] = jnp.where(rows == 0, scale, mark)
        for j in (1, 2, 3):
            start(("low", n, j), low.at[x, n], low.at[x, n], base + line(j))
            start(("misc", n, j), misc.at[x, n], misc.at[x, n], base + line(j))

    def wait_low(n):
        for j in (1, 2, 3):
            got("low", n, j)
            got("misc", n, j)

    loads["h0"].wait()
    loads["e0"].wait()
    wait_heads("h0")
    gather_line(0)
    wait_heads("e0")
    gather_line(1)
    got("e1p")
    gather_heads("e1", xall.at[x, 3, own], xall.at[x, 3, own])
    loads["down"].wait()
    loads["up"].wait()
    for i in range(4):
        for k in range(3):
            ups[i, :, 256 * k : 256 * k + 256] = dot(up[k], sel[i]).astype(BF)
    for j in (1, 2, 3):
        start(("up", j), ups.at[line(j)], upr.at[x], base + line(j))
    upr[x] = ups[x]
    make_low(0)
    wait_heads("e1")
    gather_line(3)
    pump(1)

    def eye_column(row, size):
        r, c = iota((size, size), 0), iota((size, size), 1)
        return jnp.sum(jnp.where(r == c, row, 0.0), axis=1, keepdims=True)

    def mixer_in(n, src):
        def add(t, total):
            block = src[pl.ds(pl.multiple_of(t * 128, 128), 128), :].astype(F32)
            return total + jnp.sum(block * block, axis=0, keepdims=True)
        total = lax.fori_loop(0, 14, add, jnp.zeros((1, SEQ), F32))
        scale = lax.rsqrt(total / D + EPS)
        for t in range(14):
            block = src[128 * t : 128 * t + 128, :].astype(F32) * scale
            ubuf[:, 128 * t : 128 * t + 128] = block.T.astype(BF)

        def columns(t, carry):
            at = pl.ds(pl.multiple_of(t * 256, 256), 256)
            xbuf[:, at] = silu(dot(ubuf[...], wmix[:, at]))
            return carry
        lax.fori_loop(0, 3, columns, 0)
        xbuf[:, 768:896] = silu(dot(ubuf[...], wmix[:, 768:896]))

    def mixer_out(n):
        bc = silu(dot(ubuf[...], wio[...]))
        bias = eye_column(bias_ref[...], HEADS)
        rate = jnp.exp(eye_column(decay_ref[...], HEADS))
        dt = softplus(dot(wdt_ref[...], ubuf[...], NT) + bias)
        upper = jnp.where(iota((128, 128), 0) <= iota((128, 128), 1), 1.0, 0.0)
        cum = lax.dot_general(
            dt * rate, upper, (((1,), (0,)), ((), ())), precision=HIGH, preferred_element_type=F32
        )
        cbuf[...] = jnp.zeros_like(cbuf)
        cbuf[0:HEADS, :] = cum
        cum_t = cbuf[...].T
        lanes = iota((128, 128), 1)
        rolled = pltpu.roll(bc, 64, axis=1)
        inner = lax.dot_general(
            jnp.where(lanes < 64, rolled, 0.0), jnp.where(lanes < 64, bc, 0.0), NT,
            precision=HIGH, preferred_element_type=F32,
        )
        causal = iota((128, 128), 0) >= lanes
        for pair in range(HEADS // 2):
            mixes = []
            for j in (2 * pair, 2 * pair + 1):
                gap = jnp.where(causal, cum[j : j + 1, :] - cum_t[:, j : j + 1], -1e30)
                mixes.append((inner * jnp.exp(gap) * dt[j : j + 1, :]).astype(BF))
            block = xbuf[:, 128 * pair : 128 * pair + 128]
            both = dot(jnp.concatenate(mixes, axis=0), block.astype(BF))
            skip = jnp.where(lanes < 64, skip_ref[0, 2 * pair], skip_ref[0, 2 * pair + 1])
            mixed = jnp.where(lanes < 64, both[0:128], both[128:256]) + skip * block
            ybuf[:, 128 * pair : 128 * pair + 128] = mixed.astype(BF)

        def columns(t, carry):
            at = pl.ds(pl.multiple_of(t * 256, 256), 256)
            part = dot(ybuf[...], wom[:, at])
            pbuf[pl.ds(pl.multiple_of(t * 256, 256), 128), :] = part[:, 0:128].T
            pbuf[pl.ds(pl.multiple_of(t * 256 + 128, 128), 128), :] = part[:, 128:256].T
            return carry
        lax.fori_loop(0, 7, columns, 0)
        for j in (1, 2, 3):
            at = pl.ds(pl.multiple_of(sib(j) * Q, Q), Q)
            rss[n, j - 1] = pbuf[at, :].astype(BF)
            start(("rs", n, j), rss.at[n, j - 1], rsr.at[n, j - 1], None, sib(j))

    def mixer_sum(n, src):
        total = src[own, :].astype(F32) + pbuf[own, :]
        for j in (1, 2, 3):
            got("rs", n, j)
            total = total + rsr[n, j - 1].astype(F32)
        outq[n] = total.astype(BF)

    loads["wmix"].wait()
    loads["wio"].wait()
    loads["wom"].wait()
    mixer_in(0, xall.at[x, 0])
    share_line(0)
    share_line(1)
    pump(2)
    mixer_out(0)
    mixer_sum(0, xall.at[x, 0])

    pass_on("h1p", outq.at[0], xall.at[x_next, 2, own])

    wait_low(0)
    for j in (1, 2, 3):
        got("up", j)
    marks = [misc[c, 0, 1:2, :] for c in range(3)]
    marks_bf = [m.astype(BF) for m in marks]
    identity = jnp.where(iota((128, 128), 0) == iota((128, 128), 1), 1.0, 0.0).astype(BF)

    def pick(values, masks):
        return values[0] * masks[0] + values[1] * masks[1] + values[2] * masks[2]

    def spread(n):
        def body(t, carry):
            part = t // 8
            at = pl.ds(pl.multiple_of((t - 8 * part) * 224, 224), 224)
            first = pick([xall[c, 2 * n + part, at, :] for c in range(3)], marks_bf)
            xs[n, t, 0:128, :] = dot(identity, first, NT).astype(BF)
            xs[n, t, 128:256, :] = dot(identity, xall[3, 2 * n + part, at, :], NT).astype(BF)
            return carry
        lax.fori_loop(0, 16, body, 0)

    wait_share(0)
    wait_share(1)
    spread(0)
    pump(3)
    got("h1p")
    gather_heads("h1", xall.at[x, 2, own], xall.at[x, 2, own])
    share_line(3)

    def project(n, other, dz):
        zz, yy = lax.rem(z + dz + 8, 8), (1 - y) if other else y
        acc[n] += dot(xs[n, 2 * zz + yy], wg[zz, yy, 0:224, :])

    acc[0] = jnp.zeros((256, 768), F32)
    for dz in (0, 1, -1, 2, -2, 3, -3):
        project(0, 0, dz)
    pump(4)
    project(0, 1, 0)
    project(0, 1, 1)
    project(0, 1, 2)
    project(0, 1, -2)
    wait_heads("h1")
    gather_line(2)
    make_low(1)
    pump(5)
    project(0, 1, 3)
    project(0, 1, -3)
    pump(6)
    project(0, 1, -1)
    project(0, 0, 4)
    project(0, 1, 4)

    def attend(n):
        up_first = pick([upr[c] for c in range(3)], [m[:, 0:1] for m in marks_bf])
        low_first = pick([low[c, n] for c in range(3)], marks_bf)
        scale_first = pick([misc[c, n, 0:1, :] for c in range(3)], marks)
        causal = iota((128, 128), 0) >= iota((128, 128), 1)
        for slot in (0, 1):
            low_t = low_first if slot == 0 else low[3, n]
            up_slot = up_first if slot == 0 else upr[3]
            scale = eye_column(scale_first if slot == 0 else misc[3, n, 0:1, :], 128)
            rows = slice(128 * slot, 128 * slot + 128)
            proj = (acc[n, rows, :] * scale + dot(low_t, up_slot, TN)).astype(BF)
            query, keys, values = proj[:, 0:256], proj[:, 256:512], proj[:, 512:768]
            scores = dot(query, keys, NT) * HEAD_WIDTH ** (-0.5)
            scores = jnp.where(causal, scores, -1e30)
            expd = jnp.exp(scores - jnp.max(scores, axis=-1, keepdims=True))
            probs = (expd / jnp.sum(expd, axis=-1, keepdims=True)).astype(BF)
            mx[n, x, rows, :] = dot(probs, values).astype(BF)
        for j in (1, 2, 3):
            ref = mx.at[n, x]
            start(("mx", n, j), ref, ref, base + line(j))

    attend(0)

    def unpack(t, carry):
        zz = t // 2
        yy = t - 2 * zz
        at = pl.multiple_of(t * 32, 32)
        wog[pl.ds(at, 32), 0:768] = wg[zz, yy, 224:256, :]
        wog[pl.ds(at, 16), 768:1024] = wg[zz, yy, 256:272, 0:256]
        wog[pl.ds(at + 16, 16), 768:1024] = wg[zz, yy, 256:272, 256:512]
        return carry
    lax.fori_loop(0, 16, unpack, 0)

    pt = {}

    def out_project(n):
        for j in (1, 2, 3):
            got("mx", n, j)
        for q in range(4):
            rows = slice(128 * q, 128 * q + 128)
            total = dot(wog[rows, 0:256], mx[n, 0], NT)
            for i in (1, 2, 3):
                total = total + dot(wog[rows, 256 * i : 256 * i + 256], mx[n, i], NT)
            rs2s[n, q] = total.astype(BF)
        for j in (1, 2, 3):
            start(("rs2", n, j), rs2s.at[n, sib(j)], rs2r.at[n, j - 1], None, sib(j))

    def send_attn(n):
        total = rs2s[n, h].astype(F32)
        for j in (1, 2, 3):
            got("rs2", n, j)
            total = total + rs2r[n, j - 1].astype(F32)
        atb[n, 0] = total[:, 0:128].astype(BF)
        atb[n, 1] = total[:, 128:256].astype(BF)
        for j in (1, 2, 3):
            start(("at", n, j), atb.at[n, line(j) // 3], atr.at[n, x], base + line(j))
        atr[n, x] = atb[n, x // 3]

    def make_middle(n):
        for j in (1, 2, 3):
            got("at", n, j)
        r, c = iota((224, 256), 0), iota((224, 256), 1)
        home = (4 * ((c >> 5) & 1) + (c >> 6)) * 28 + (c & 31)
        order = jnp.where((r == home) & ((c & 31) < 28), 1.0, 0.0).astype(BF)
        for half in (0, 1):
            stack = jnp.concatenate([atr[n, i, 64 * half : 64 * half + 64, :] for i in range(4)], axis=0)
            at = pl.ds(pl.multiple_of(h * Q + 224 * half, 224), 224)
            mid[n, at, :] = (xall[x, 2 * n, at, :].astype(F32) + dot(order, stack)).astype(BF)
        gather_heads(("mid", n), mid.at[n, own], mid.at[n, own])

    mark_here = calls_ref[0].astype(F32)

    def choose(n, plain):
        wait_heads(("mid", n))

        def body(t, carry):
            at = pl.ds(pl.multiple_of(t * 128, 128), 128)
            called = mid[n, at, :].astype(F32)
            mbuf[n, at, :] = (called * mark_here + plain[at, :].astype(F32) * (1.0 - mark_here)).astype(BF)
            return carry
        lax.fori_loop(0, 14, body, 0)

    share_line(2)
    out_project(0)
    wait_share(3)
    wait_share(2)
    wait_low(1)
    send_attn(0)
    spread(1)
    make_middle(0)
    acc[1] = jnp.zeros((256, 768), F32)

    def project_all(t, carry):
        zz = t // 2
        acc[1] += dot(xs[1, t], wg[zz, t - 2 * zz, 0:224, :])
        return carry
    lax.fori_loop(0, 16, project_all, 0)
    attend(1)
    choose(0, xall.at[x, 0])
    mixer_in(1, mbuf.at[0])
    mixer_out(1)
    out_project(1)
    mixer_sum(1, mbuf.at[0])

    pass_on("hfp", outq.at[1], hf.at[own])

    save0 = pltpu.make_async_copy(outq.at[1], out_ref.at[0], load_sem.at[10])
    save0.start()
    send_attn(1)
    make_middle(1)
    got("hfp")
    gather_heads("hf", hf.at[own], hf.at[own])
    wait_heads("hf")
    choose(1, hf)
    mixer_in(2, mbuf.at[1])
    mixer_out(2)
    mixer_sum(2, mbuf.at[1])
    save1 = pltpu.make_async_copy(outq.at[2], out_ref.at[1], load_sem.at[11])
    save1.start()
    for desc in descs.values():
        desc.wait_send()
    save0.wait()
    save1.wait()


def on_device(
    entering_hidden, entering_embed, incoming_embed, mixer_input_weight,
    input_output_matrix_weight, step_size_weight, mixer_output_weight, log_decay_rate,
    step_size_bias, skip_weight, shared_query_key_value, shared_output_weight, adapter_down,
    adapter_upward, calls,
):
    flip = lambda v: jnp.swapaxes(v, 1, 2)[0]
    hbm = pl.BlockSpec(memory_space=pl.ANY)
    vmem = pl.BlockSpec(memory_space=pltpu.VMEM)
    smem = pl.BlockSpec(memory_space=pltpu.SMEM)
    scratch = [
        ((4, 4, D, SEQ), BF),
        ((2, 16, 256, 224), BF),
        ((8, 2, 272, 768), BF),
        ((D, 896), BF),
        ((D, 128), BF),
        ((896, D), BF),
        ((2 * D, 128), BF),
        ((3, 128, 896), BF),
        ((3, 56, 896), BF),
        ((4, 896, 256), BF),
        ((4, 64, 768), BF),
        ((4, 64, 768), BF),
        ((32, 896), BF),
        ((4, 128, 768), BF),
        ((4, 128, 768), BF),
        ((4, 2, 128, 128), BF),
        ((4, 2, 8, 128), F32),
        ((2, 256, 768), F32),
        ((512, 1024), BF),
        ((2, 4, 256, 256), BF),
        ((2, 4, 128, 256), BF),
        ((2, 3, 128, 256), BF),
        ((2, 2, 128, 128), BF),
        ((2, 4, 128, 128), BF),
        ((2, D, SEQ), BF),
        ((D, SEQ), BF),
        ((2, D, SEQ), BF),
        ((SEQ, D), BF),
        ((SEQ, 896), BF),
        ((SEQ, 896), F32),
        ((D, SEQ), F32),
        ((128, 128), F32),
        ((3, 3, Q, SEQ), BF),
        ((3, 3, Q, SEQ), BF),
        ((3, Q, SEQ), BF),
    ]
    out = pl.pallas_call(
        kernel,
        out_shape=jax.ShapeDtypeStruct((2, Q, SEQ), BF),
        in_specs=[
            hbm, hbm, hbm, hbm, hbm, vmem, hbm, vmem, vmem, smem, hbm, vmem, hbm, hbm, smem,
        ],
        out_specs=hbm,
        scratch_shapes=[pltpu.VMEM(shape, dtype) for shape, dtype in scratch]
        + [
            pltpu.SemaphoreType.DMA((SENDS,)),
            pltpu.SemaphoreType.DMA((SENDS,)),
            pltpu.SemaphoreType.DMA((12,)),
        ],
        compiler_params=pltpu.CompilerParams(
            collective_id=0, has_side_effects=True, vmem_limit_bytes=58 * 1024 * 1024
        ),
    )(
        flip(entering_hidden), flip(entering_embed), flip(incoming_embed), mixer_input_weight[0],
        input_output_matrix_weight[0], flip(step_size_weight), mixer_output_weight[0],
        log_decay_rate, step_size_bias, skip_weight,
        jnp.swapaxes(shared_query_key_value, 0, 1), shared_output_weight, adapter_down[0],
        jnp.swapaxes(adapter_upward[0], 0, 1), calls,
    )
    return jnp.swapaxes(out, 1, 2)[:, None]


def solution(mesh):
    in_specs = (
        P("section", None, "head"),
        P("section", None, "head"),
        P(None, None, "head"),
        P("section", None, "head"),
        P("section", None, None),
        P("section", None, "head"),
        P("section", "head", None),
        P("section", "head"),
        P("section", "head"),
        P("section", "head"),
        P("section", None, "head"),
        P("section", "head"),
        P("section", None, None),
        P("section", None, None, "head"),
        P("section"),
    )
    out_specs = P(None, "section", None, "head")
    return jax.shard_map(
        on_device, mesh=mesh, in_specs=in_specs, out_specs=out_specs, check_vma=False
    )
```

```python
import jax
import jax.numpy as jnp
from jax import lax
from jax.experimental import pallas as pl
from jax.experimental.pallas import tpu as pltpu
from jax.sharding import PartitionSpec as P

MESH = pl.DeviceIdType.MESH
BF = jnp.bfloat16
F32 = jnp.float32
NT = (((1,), (1,)), ((), ()))
TN = (((0,), (0,)), ((), ()))
HIGH = lax.Precision.HIGHEST
D = 1792
Q = 448
SEQ = 128
HEADS = 14
HEAD_WIDTH = 224
EPS = 1e-05
SENDS = 160
POOL = 48


def iota(shape, dim):
    return lax.broadcasted_iota(jnp.int32, shape, dim)


def dot(a, b, dims=(((1,), (0,)), ((), ()))):
    return lax.dot_general(a, b, dims, preferred_element_type=F32)


def silu(v):
    return v / (1.0 + jnp.exp(-v))


def softplus(v):
    return jnp.maximum(v, 0.0) + jnp.log(1.0 + jnp.exp(-jnp.abs(v)))


def kernel(
    h0_in, e0_in, inc_in, wmix_in, wio_in, wdt_ref, wom_in, decay_ref, bias_ref, skip_ref,
    qkv_in, wo_ref, down_in, up_in, calls_ref,
    out_ref,
    xall, xs, wg, wr, rep, lane, wmix, wio, wom, down, up, qw, sel, a2s, a2r, ups, upr, upf, low, misc,
    acc, wog, wo32, mx, rs2s, rs2p, rs2m, atb, atr, mid, hf, mbuf, ubuf, ybuf, xbuf, pbuf, cbuf, rss,
    rsp, rsm,
    outq, send_sem, recv_sem, load_sem,
):
    s = lax.axis_index("section")
    h = lax.axis_index("head")
    x = lax.rem(s, 4)
    y = lax.rem(s // 4, 2)
    z = s // 8
    core = lax.rem(h, 2)
    base = s - x
    sec_up = lax.rem(z + 1, 8) * 8 + lax.rem(s, 8)
    sec_down = lax.rem(z + 7, 8) * 8 + lax.rem(s, 8)
    sec_y = s + 4 - 8 * y
    sec_next = lax.rem(s + 1, 64)
    sec_prev = lax.rem(s + 63, 64)
    x_next = lax.rem(x + 1, 4)
    x_prev = lax.rem(x + 3, 4)
    x_far = lax.rem(x + 2, 4)
    twin = h + 1 - 2 * core
    mate = lax.rem(h + 2, 4)
    far = lax.rem(twin + 2, 4)

    def line(j):
        return lax.rem(x + j, 4)

    index = {}
    descs = {}
    sends = {}

    def only(cond, act):
        if cond is None:
            act()
        else:
            pl.when(cond)(lambda: act())

    pool = {}

    def remote(key, src, dst, section, head):
        at = index.setdefault(key, len(index))
        slot = at % POOL
        before = pool.get(slot)
        if before != key:
            if before is not None:
                only(sends[before], descs[before].wait_send)
            pool[slot] = key
        return pltpu.make_async_remote_copy(
            src_ref=src, dst_ref=dst, send_sem=send_sem.at[slot], recv_sem=recv_sem.at[at],
            device_id={"section": section, "head": head}, device_id_type=MESH,
        )

    def start(key, src, dst, section=None, head=None, cond=None):
        descs[key] = remote(key, src, dst, s if section is None else section, h if head is None else head)
        sends[key] = cond
        only(cond, descs[key].start)

    def pass_on(name, src, dst):
        for key, head in (((name, "same"), h), ((name, "mate"), mate)):
            fresh = remote(key, inc_in, dst, sec_next, head)
            descs[key] = remote(key, src, dst, sec_next, head)
            sends[key] = None
            pl.when(s == 63)(fresh.start)
            pl.when(s != 63)(descs[key].start)

    def pass_got(name, buf_at):
        got(name, "same")
        got(name, "mate")
        for key, rows in (((name, "own"), own), ((name, "other"), rows_of(mate))):
            ref = buf_at(rows)
            start(key, ref, ref, None, twin)

    def pass_wait(name):
        got(name, "own")
        got(name, "other")

    def got(*key, cond=None):
        only(cond, descs[key].wait_recv)

    loads = {}

    def load(name, src, dst):
        loads[name] = pltpu.make_async_copy(src, dst, load_sem.at[len(loads)])
        loads[name].start()

    def rows_of(head):
        return pl.ds(pl.multiple_of(head * Q, Q), Q)

    own = rows_of(h)
    load("qkv", qkv_in, qw)
    load("h0", h0_in, xall.at[x, 0, own])
    load("e0", e0_in, xall.at[x, 1, own])
    load("down", down_in, down)
    load("up", up_in, up)
    load("wmix", wmix_in, wmix)
    load("wio", wio_in, wio)
    load("wom", wom_in, wom)

    barrier = pltpu.get_barrier_semaphore()
    peers = [(base + line(j), h) for j in (1, 2, 3)] + [(s, twin), (s, mate)]
    peers += [(sec_up, h), (sec_down, h), (sec_y, h), (sec_next, h), (sec_prev, h)]
    peers += [(sec_next, mate), (sec_prev, mate)]
    for section, head in peers:
        pl.semaphore_signal(
            barrier, inc=1, device_id={"section": section, "head": head}, device_id_type=MESH
        )
    for i in range(4):
        r, c = iota((896, 256), 0), iota((896, 256), 1)
        sel[i] = jnp.where((r == c + 224 * i) & (c < 224), 1.0, 0.0).astype(BF)
    wo32[...] = jnp.zeros_like(wo32)
    wo32[0:28, :] = wo_ref[...]
    k, c = iota((224, 64), 0), iota((224, 64), 1)
    rep[...] = jnp.where(((k - c) == 56 * ((k >= 56) * 1 + (k >= 112) * 1 + (k >= 168) * 1)) & (c < 56), 1.0, 0.0).astype(BF)
    k, c = iota((224, 128), 0), iota((224, 128), 1)
    lane[...] = jnp.where((c >> 5) == (k >= 56) * 1 + (k >= 112) * 1 + (k >= 168) * 1, 1.0, 0.0).astype(BF)

    def tiles(query, keys, values):
        at = iota((query.shape[0], 128), 1)
        rest = values[:, 128:256]
        return [
            query[:, 0:128],
            keys[:, 0:128],
            values[:, 0:128],
            jnp.where(at < 96, query[:, 128:256], pltpu.roll(rest, 96, axis=1)),
            jnp.where(at < 96, keys[:, 128:256], pltpu.roll(rest, 64, axis=1)),
            jnp.where((at >= 64) & (at < 96), rest, 0.0),
        ]

    loads["qkv"].wait()
    for i in range(4):
        cut = tiles(*[dot(qw[k], sel[i]) for k in range(3)])
        turned = [pltpu.roll(cut[5], shift, axis=1) for shift in (64, 96, 32)]
        cut[5] = jnp.where(
            x == 0, turned[0], jnp.where(x == 1, turned[1], jnp.where(x == 2, cut[5], turned[2]))
        )
        for t in range(6):
            block = jnp.concatenate([cut[t], jnp.zeros((8, 128), F32)], axis=0)
            a2s[i, :, 128 * t : 128 * t + 128] = block.astype(BF)
    pl.semaphore_wait(barrier, len(peers))

    def heads_start(name, src, dst, cond=None):
        start((name, "mate"), src, dst, None, mate, cond)
        start((name, "twin"), src, dst, None, twin, cond)

    def heads_pass(name, buf_at, cond=None):
        got(name, "mate", cond=cond)
        ref = buf_at(rows_of(mate))
        start((name, "pass"), ref, ref, None, twin, cond)

    def heads_wait(name, cond=None):
        got(name, "twin", cond=cond)
        got(name, "pass", cond=cond)

    for j in (1, 2, 3):
        start(("a2a", j), a2s.at[line(j)], a2r.at[x], base + line(j))
    heads_start("h0", h0_in, xall.at[x, 0, own])
    heads_start("e0", e0_in, xall.at[x, 1, own])
    first = x == 0
    fresh = remote(("e1p",), inc_in, xall.at[0, 3, own], sec_next, h)
    descs[("e1p",)] = remote(("e1p",), e0_in, xall.at[0, 3, own], sec_next, h)
    sends[("e1p",)] = x == 3
    pl.when(s == 63)(fresh.start)
    pl.when((x == 3) & (s != 63))(descs[("e1p",)].start)
    a2r[x] = a2s[x]
    r, c = iota((224, 256), 0), iota((224, 256), 1)
    compact = jnp.where(((c - 8 * (c >> 6)) == r) & ((c & 63) < 56), 1.0, 0.0).astype(BF)
    for j in (1, 2, 3):
        got("a2a", j)
    packed = jnp.concatenate([a2r[c, :, 0:640] for c in range(4)], axis=0)
    wg[z, y, 0:224, :] = dot(compact, packed).astype(BF)
    rest = (a2r[0, :, 640:768] + a2r[1, :, 640:768]) + (a2r[2, :, 640:768] + a2r[3, :, 640:768])
    for g in range(4):
        wg[z, y, 224:240, 128 * g : 128 * g + 128] = rest[16 * g : 16 * g + 16]
    wg[z, y, 224:240, 512:640] = jnp.zeros((16, 128), BF)
    wg[z, y, 240:272, :] = wo32[:, 0:640]
    wg[z, y, 272:288, 0:256] = wo32[0:16, 640:896]
    wg[z, y, 272:288, 256:512] = wo32[16:32, 640:896]
    wg[z, y, 272:288, 512:640] = jnp.zeros((16, 128), BF)

    spans = {"all": (0, 288), "w": (0, 240), "w0": (0, 128), "w1": (128, 112), "o": (240, 48)}

    def push(way, other, dz, span="all"):
        first_row, rows = spans[span]
        zz, yy = lax.rem(z + dz + 8, 8), (1 - y) if other else y
        ref = wg.at[zz, yy, pl.ds(first_row, rows)]
        section = {"down": sec_down, "up": sec_up, "y": sec_y}[way]
        start((way, other, dz, span), ref, ref, section)

    def here(way, other, dz, span="all"):
        got(way, other, dz, span)

    def pump(step):
        if step == 0:
            push("down", 0, 0)
            push("up", 0, 0)
            push("y", 0, 0)
        if step == 1:
            here("down", 0, 0)
            push("down", 0, 1)
            push("y", 0, 1)
            here("up", 0, 0)
            push("up", 0, -1)
        if step == 2:
            here("down", 0, 1)
            push("down", 0, 2)
            push("y", 0, 2, "w0")
            here("up", 0, -1)
            push("up", 0, -2)
            push("y", 0, -2, "w1")
            push("y", 0, 2, "w1")
            push("y", 0, -2, "w0")
            push("y", 0, -1, "w")
            for dz in (2, -2, -1):
                push("y", 0, dz, "o")
        if step == 3:
            here("down", 0, 2)
            push("down", 0, 3, "w0")
            here("up", 0, -2)
            push("up", 0, -3, "w1")
        if step == 4:
            here("y", 0, 0)
            here("y", 0, 1)
            here("y", 0, 2, "w0")
            push("down", 1, 2, "w0")
        if step == 5:
            here("y", 0, -2, "w1")
            push("up", 1, -2, "w1")
        if step == 6:
            here("y", 0, 2, "w1")
            push("down", 1, 2, "w1")
        if step == 7:
            here("y", 0, -2, "w0")
            push("up", 1, -2, "w0")
        if step == 8:
            here("down", 1, 2, "w0")
            push("down", 1, 3, "w0")
            here("up", 1, -2, "w1")
            push("up", 1, -3, "w1")
            push("down", 0, 3, "o")
        if step == 9:
            here("y", 0, 2, "o")
            push("down", 1, 2, "o")
            here("y", 0, -2, "o")
            push("up", 1, -2, "o")
        if step == 10:
            here("down", 1, 2, "o")
            push("down", 1, 3, "o")
        if step == 11:
            here("y", 0, -1, "o")
            here("down", 0, 3, "o")
            here("up", 1, -2, "o")
            here("down", 1, 3, "o")

    def unpack(t, carry):
        zz = t // 2
        yy = t - 2 * zz
        at = pl.multiple_of(t * 32, 32)
        wog[pl.ds(at, 32), 0:640] = wg[zz, yy, 240:272, :]
        wog[pl.ds(at, 16), 640:896] = wg[zz, yy, 272:288, 0:256]
        wog[pl.ds(at + 16, 16), 640:896] = wg[zz, yy, 272:288, 256:512]
        return carry

    def line_rows(first, count):
        return pl.ds(pl.multiple_of(core * 896 + first, Q), count)

    def line_start(n):
        ref = xall.at[x, n, line_rows(0, 896)]
        start(("line", n, "next"), ref, ref, base + x_next)
        start(("line", n, "prev"), ref, ref, base + x_prev)

    def line_pass(n):
        got("line", n, "next")
        ref = xall.at[x_prev, n, line_rows(0, 448)]
        start(("line2", n, "next"), ref, ref, base + x_next)
        got("line", n, "prev")
        ref = xall.at[x_next, n, line_rows(448, 448)]
        start(("line2", n, "prev"), ref, ref, base + x_prev)
        for at, key in ((x_prev, 1), (x_next, 2)):
            ref = xall.at[at, n, line_rows(0, 896)]
            start(("share", n, key), ref, ref, None, twin)

    def line_share(n):
        got("line2", n, "next")
        got("line2", n, "prev")
        ref = xall.at[x_far, n, line_rows(0, 896)]
        start(("share", n, 3), ref, ref, None, twin)

    def line_first():
        whole = xall.at[0, 3, line_rows(0, 896)]
        start(("le", "next"), whole, whole, base + 1, None, first)
        start(("le", "prev"), whole, whole, base + 3, None, first)

    def line_first_pass():
        whole = xall.at[0, 3, line_rows(0, 896)]
        for key, at, rows in (("next", 1, line_rows(0, 448)), ("prev", 3, line_rows(448, 448))):
            got("le", key, cond=x == at)
            part = xall.at[0, 3, rows]
            start(("le2", key), part, part, base + 2, None, x == at)
        start(("le", "side"), whole, whole, None, twin, (x == 1) | (x == 3))

    def line_first_share():
        whole = xall.at[0, 3, line_rows(0, 896)]
        for key in ("next", "prev"):
            got("le2", key, cond=x == 2)
        start(("le", "far"), whole, whole, None, twin, x == 2)

    def line_first_wait():
        got("le", "side", cond=(x == 1) | (x == 3))
        got("le", "far", cond=x == 2)

    def line_wait(n):
        for key in (1, 2, 3):
            got("share", n, key)

    def state(c, n):
        if n != 3:
            return c, n
        if isinstance(c, int):
            return (c - 1, 1) if c else (0, 3)
        return jnp.maximum(c - 1, 0), jnp.where(c == 0, 3, 1)

    def row_scale(n):
        total = jnp.zeros((1, SEQ), F32)
        for part in (0, 1):
            def add(t, total):
                block = xall[*state(x, 2 * n + part), pl.ds(pl.multiple_of(t * 128, 128), 128), :].astype(F32)
                return total + jnp.sum(block * block, axis=0, keepdims=True)
            total = lax.fori_loop(0, 14, add, total)
        return lax.rsqrt(total / (2 * D) + EPS)

    def make_low(n):
        scale = row_scale(n)
        total = jnp.zeros((128, SEQ), F32)
        for part in (0, 1):
            total = total + dot(down[part * D : part * D + D, :], xall[*state(x, 2 * n + part)], TN)
        low[x, n] = (total * scale).astype(BF)
        rows = iota((8, 128), 0)
        mark = calls_ref[0].astype(F32)
        misc[x, n] = jnp.where(rows == 0, scale, mark)
        for j in (1, 2, 3):
            start(("low", n, j), low.at[x, n], low.at[x, n], base + line(j))
            start(("misc", n, j), misc.at[x, n], misc.at[x, n], base + line(j))

    def pack_up():
        for i in range(4):
            cut = tiles(*[dot(up[k], sel[i]) for k in range(3)])
            for t in range(6):
                ups[i, :, 128 * t : 128 * t + 128] = cut[t].astype(BF)
        start(("up", "hop"), ups.at[x_far, 64:128], upf, base + x_prev)
        start(("up", "next"), ups.at[x_next], upr.at[x], base + x_next)
        start(("up", "prev"), ups.at[x_prev], upr.at[x], base + x_prev)
        start(("up", "far"), ups.at[x_far, 0:64], upr.at[x, 0:64], base + x_far)
        upr[x] = ups[x]

    def up_pass():
        got("up", "hop")
        start(("up", "last"), upf, upr.at[x_next, 64:128], base + x_prev)

    def up_wait():
        for key in ("next", "prev", "far", "last"):
            got("up", key)

    def wait_low(n):
        for j in (1, 2, 3):
            got("low", n, j)
            got("misc", n, j)

    def eye_column(row, size):
        r, c = iota((size, size), 0), iota((size, size), 1)
        return jnp.sum(jnp.where(r == c, row, 0.0), axis=1, keepdims=True)

    def mixer_in(n, src):
        def add(t, total):
            block = src[pl.ds(pl.multiple_of(t * 128, 128), 128), :].astype(F32)
            return total + jnp.sum(block * block, axis=0, keepdims=True)
        total = lax.fori_loop(0, 14, add, jnp.zeros((1, SEQ), F32))
        scale = lax.rsqrt(total / D + EPS)
        for t in range(14):
            block = src[128 * t : 128 * t + 128, :].astype(F32) * scale
            ubuf[:, 128 * t : 128 * t + 128] = block.T.astype(BF)

        def columns(t, carry):
            at = pl.ds(pl.multiple_of(t * 256, 256), 256)
            xbuf[:, at] = silu(dot(ubuf[...], wmix[:, at]))
            return carry
        lax.fori_loop(0, 3, columns, 0)
        xbuf[:, 768:896] = silu(dot(ubuf[...], wmix[:, 768:896]))

    def mixer_out(n, between=None):
        bc = silu(dot(ubuf[...], wio[...]))
        bias = eye_column(bias_ref[...], HEADS)
        rate = jnp.exp(eye_column(decay_ref[...], HEADS))
        dt = softplus(dot(wdt_ref[...], ubuf[...], NT) + bias)
        upper = jnp.where(iota((128, 128), 0) <= iota((128, 128), 1), 1.0, 0.0)
        cum = lax.dot_general(
            dt * rate, upper, (((1,), (0,)), ((), ())), precision=HIGH, preferred_element_type=F32
        )
        cbuf[...] = jnp.zeros_like(cbuf)
        cbuf[0:HEADS, :] = cum
        cum_t = cbuf[...].T
        lanes = iota((128, 128), 1)
        rolled = pltpu.roll(bc, 64, axis=1)
        inner = lax.dot_general(
            jnp.where(lanes < 64, rolled, 0.0), jnp.where(lanes < 64, bc, 0.0), NT,
            precision=HIGH, preferred_element_type=F32,
        )
        causal = iota((128, 128), 0) >= lanes
        for pair in range(HEADS // 2):
            mixes = []
            for j in (2 * pair, 2 * pair + 1):
                gap = jnp.where(causal, cum[j : j + 1, :] - cum_t[:, j : j + 1], -1e30)
                mixes.append((inner * jnp.exp(gap) * dt[j : j + 1, :]).astype(BF))
            block = xbuf[:, 128 * pair : 128 * pair + 128]
            both = dot(jnp.concatenate(mixes, axis=0), block.astype(BF))
            skip = jnp.where(lanes < 64, skip_ref[0, 2 * pair], skip_ref[0, 2 * pair + 1])
            mixed = jnp.where(lanes < 64, both[0:128], both[128:256]) + skip * block
            ybuf[:, 128 * pair : 128 * pair + 128] = mixed.astype(BF)
        if between is not None:
            between()

        def columns(t, carry):
            at = pl.ds(pl.multiple_of(t * 256, 256), 256)
            part = dot(ybuf[...], wom[:, at])
            pbuf[pl.ds(pl.multiple_of(t * 256, 256), 128), :] = part[:, 0:128].T
            pbuf[pl.ds(pl.multiple_of(t * 256 + 128, 128), 128), :] = part[:, 128:256].T
            return carry
        lax.fori_loop(0, 7, columns, 0)
        rss[n, 0] = pbuf[rows_of(twin), :].astype(BF)
        rss[n, 1] = pbuf[rows_of(far), :].astype(BF)
        start(("rs", n, "twin"), rss.at[n], rsp.at[n], None, twin)

    def mixer_pass(n):
        got("rs", n, "twin")
        rsm[n, 0] = (pbuf[rows_of(mate), :] + rsp[n, 1].astype(F32)).astype(BF)
        start(("rs", n, "mate"), rsm.at[n, 0], rsm.at[n, 1], None, mate)

    def mixer_sum(n, src):
        total = src[own, :].astype(F32) + pbuf[own, :] + rsp[n, 0].astype(F32)
        got("rs", n, "mate")
        outq[n] = (total + rsm[n, 1].astype(F32)).astype(BF)

    def marks():
        return [misc[c, 0, 1:2, :] for c in range(3)]

    def marks_bf():
        return [m.astype(BF) for m in marks()]

    identity = jnp.where(iota((128, 128), 0) == iota((128, 128), 1), 1.0, 0.0).astype(BF)

    def pick(values, masks):
        return values[0] * masks[0] + values[1] * masks[1] + values[2] * masks[2]

    def spread(n, parts=(0, 1)):
        for part in parts:
            places = [state(c, 2 * n + part) for c in range(4)]

            def body(t, carry, part=part, places=places):
                at = pl.ds(pl.multiple_of(t * 224, 224), 224)
                chosen = pick([xall[*places[c], at, :] for c in range(3)], marks_bf())
                xs[n, 8 * part + t, 0:128, :] = dot(identity, chosen, NT).astype(BF)
                xs[n, 8 * part + t, 128:256, :] = dot(identity, xall[*places[3], at, :], NT).astype(BF)
                return carry
            lax.fori_loop(0, 8, body, 0)

    def project(n, other, dz):
        zz, yy = lax.rem(z + dz + 8, 8), (1 - y) if other else y
        rest = jnp.concatenate([wg[zz, yy, 224:240, 128 * g : 128 * g + 128] for g in range(4)], axis=0)
        wr[zz, yy] = (dot(rep[...], rest) * lane[...].astype(F32)).astype(BF)
        project_piece(n, zz, yy)

    def project_piece(n, zz, yy):
        rows = xs[n, 2 * zz + yy]
        acc[n, :, 0:640] += dot(rows, wg[zz, yy, 0:224, :])
        acc[n, :, 640:768] += dot(rows, wr[zz, yy])

    def attend(n):
        up_first = pick([upr[c] for c in range(3)], [m[:, 0:1] for m in marks_bf()])
        low_first = pick([low[c, n] for c in range(3)], marks_bf())
        scale_first = pick([misc[c, n, 0:1, :] for c in range(3)], marks())
        causal = iota((128, 128), 0) >= iota((128, 128), 1)
        for slot in (0, 1):
            low_t = low_first if slot == 0 else low[3, n]
            up_slot = up_first if slot == 0 else upr[3]
            scale = eye_column(scale_first if slot == 0 else misc[3, n, 0:1, :], 128)
            rows = slice(128 * slot, 128 * slot + 128)
            total = acc[n, rows, :] * scale
            rest = total[:, 640:768]
            rest = rest + pltpu.roll(rest, 64, axis=1)
            rest = rest + pltpu.roll(rest, 32, axis=1)
            delta = dot(low_t, up_slot, TN)
            proj = [total[:, 128 * t : 128 * t + 128] + delta[:, 128 * t : 128 * t + 128] for t in range(5)]
            proj.append(rest + delta[:, 640:768])
            at = iota((128, 128), 1)
            tail = jnp.where(
                at < 32,
                pltpu.roll(proj[3], 32, axis=1),
                jnp.where(at < 64, pltpu.roll(proj[4], 64, axis=1), jnp.where(at < 96, proj[5], 0.0)),
            )
            query = jnp.concatenate([proj[0], jnp.where(at < 96, proj[3], 0.0)], axis=1).astype(BF)
            keys = jnp.concatenate([proj[1], jnp.where(at < 96, proj[4], 0.0)], axis=1).astype(BF)
            values = jnp.concatenate([proj[2], tail], axis=1).astype(BF)
            scores = dot(query, keys, NT) * HEAD_WIDTH ** (-0.5)
            scores = jnp.where(causal, scores, -1e30)
            expd = jnp.exp(scores - jnp.max(scores, axis=-1, keepdims=True))
            probs = (expd / jnp.sum(expd, axis=-1, keepdims=True)).astype(BF)
            mixed = dot(probs, values)
            at = pl.multiple_of(224 * x, 32)
            mx[n, pl.ds(at, 128), rows] = mixed[:, 0:128].T.astype(BF)
            mx[n, pl.ds(at + 128, 96), rows] = mixed[:, 128:256].T[0:96].astype(BF)

    def send_mixed(n):
        block = mx.at[n, pl.ds(pl.multiple_of(224 * x, 32), 224)]
        part = mx.at[n, pl.ds(pl.multiple_of(224 * x, 32), 112)]
        start(("mx", n, "prev"), block, block, base + x_prev)
        start(("mx", n, "next"), block, block, base + x_next)
        start(("mx", n, "far"), part, part, base + x_far)

    def pass_mixed(n):
        got("mx", n, "prev")
        part = mx.at[n, pl.ds(pl.multiple_of(224 * x_next + 112, 16), 112)]
        start(("mx", n, "last"), part, part, base + x_prev)

    pt = {}

    def out_project(n):
        for key in ("next", "far", "last"):
            got("mx", n, key)
        for q in range(4):
            rows = slice(128 * q, 128 * q + 128)
            rs2s[n, q] = dot(wog[rows, :], mx[n]).astype(BF)
        start(("rs2", n, 0), rs2s.at[n, twin], rs2p.at[n, 0], None, twin)
        start(("rs2", n, 1), rs2s.at[n, far], rs2p.at[n, 1], None, twin)

    def pass_attn(n):
        got("rs2", n, 1)
        rs2m[n, 0] = (rs2s[n, mate].astype(F32) + rs2p[n, 1].astype(F32)).astype(BF)
        start(("rs2", n, "mate"), rs2m.at[n, 0], rs2m.at[n, 1], None, mate)

    def send_attn(n):
        got("rs2", n, 0)
        got("rs2", n, "mate")
        total = rs2s[n, h].astype(F32) + rs2p[n, 0].astype(F32) + rs2m[n, 1].astype(F32)
        atb[n, 0] = total[:, 0:128].astype(BF)
        atb[n, 1] = total[:, 128:256].astype(BF)
        for j in (1, 2, 3):
            start(("at", n, j), atb.at[n, line(j) // 3], atr.at[n, x], base + line(j))
        atr[n, x] = atb[n, x // 3]

    def make_middle(n):
        for j in (1, 2, 3):
            got("at", n, j)
        r, c = iota((224, 256), 0), iota((224, 256), 1)
        home = (4 * ((c >> 5) & 1) + (c >> 6)) * 28 + (c & 31)
        order = jnp.where((r == home) & ((c & 31) < 28), 1.0, 0.0).astype(BF)
        for half in (0, 1):
            stack = jnp.concatenate([atr[n, i, 64 * half : 64 * half + 64, :] for i in range(4)], axis=0)
            at = pl.ds(pl.multiple_of(h * Q + 224 * half, 224), 224)
            mid[n, at, :] = (xall[x, 2 * n, at, :].astype(F32) + dot(order, stack)).astype(BF)
        heads_start("mid%d" % n, mid.at[n, own], mid.at[n, own])

    def mid_rows(n):
        return lambda rows: mid.at[n, rows]

    mark_here = calls_ref[0].astype(F32)

    def choose(n, plain):
        heads_wait("mid%d" % n)

        def body(t, carry):
            at = pl.ds(pl.multiple_of(t * 128, 128), 128)
            called = mid[n, at, :].astype(F32)
            mbuf[n, at, :] = (called * mark_here + plain[at, :].astype(F32) * (1.0 - mark_here)).astype(BF)
            return carry
        lax.fori_loop(0, 14, body, 0)

    def project_rest(part):
        def body(t, carry):
            zz = t // 2
            project_piece(1, zz, t - 2 * zz)
            return carry
        lax.fori_loop(8 * part, 8 * part + 8, body, 0)

    def state_rows(n):
        return lambda rows: xall.at[x, n, rows]

    pump(0)
    loads["h0"].wait()
    loads["e0"].wait()
    heads_pass("h0", state_rows(0))
    heads_pass("e0", state_rows(1))
    heads_wait("h0")
    line_start(0)
    heads_wait("e0")
    line_start(1)
    got("e1p", cond=first)
    e1_rows = lambda rows: xall.at[0, 3, rows]
    heads_start("e1", e1_rows(own), e1_rows(own), first)
    loads["wmix"].wait()
    mixer_in(0, xall.at[x, 0])
    loads["wio"].wait()
    loads["wom"].wait()
    mixer_out(0)
    pump(1)
    line_pass(0)
    heads_pass("e1", e1_rows, first)
    mixer_pass(0)
    loads["down"].wait()
    make_low(0)
    line_pass(1)
    heads_wait("e1", first)
    line_first()
    line_share(0)
    pump(2)
    mixer_sum(0, xall.at[x, 0])
    pass_on("h1p", outq.at[0], xall.at[x_next, 2, own])
    line_share(1)
    loads["up"].wait()
    pack_up()
    acc[0] = jnp.zeros((256, 768), F32)
    acc[1] = jnp.zeros((256, 768), F32)
    wait_low(0)
    line_wait(0)
    line_wait(1)
    spread(0, (0,))
    pump(3)
    pump(4)
    spread(0, (1,))
    pump(5)
    for dz in (0, 1, -1, 2, -2):
        project(0, 0, dz)
    up_pass()
    pump(6)
    pass_got("h1p", state_rows(2))
    line_first_pass()
    pump(7)
    project(0, 1, 0)
    project(0, 1, 1)
    pump(8)
    pass_wait("h1p")
    line_start(2)
    make_low(1)
    line_first_share()
    here("down", 0, 3, "w0")
    here("up", 0, -3, "w1")
    project(0, 0, 3)
    project(0, 0, -3)
    project(0, 0, 4)
    here("down", 1, 2, "w1")
    here("up", 1, -2, "w0")
    for dz in (2, -2, 3, -3):
        project(0, 1, dz)
    here("y", 0, -1, "w")
    project(0, 1, -1)
    here("down", 1, 3, "w0")
    here("up", 1, -3, "w1")
    project(0, 1, 4)
    up_wait()
    pump(9)
    attend(0)
    send_mixed(0)
    pump(10)
    line_pass(2)
    line_first_wait()
    spread(1, (1,))
    pass_mixed(0)
    project_rest(1)
    pump(11)
    lax.fori_loop(0, 16, unpack, 0)
    line_share(2)
    out_project(0)
    wait_low(1)
    pass_attn(0)
    line_wait(2)
    spread(1, (0,))
    project_rest(0)
    attend(1)
    send_attn(0)
    send_mixed(1)
    make_middle(0)
    pass_mixed(1)
    heads_pass("mid0", mid_rows(0))
    out_project(1)
    choose(0, xall.at[x, 0])
    mixer_in(1, mbuf.at[0])
    pass_attn(1)
    mixer_out(1)
    mixer_pass(1)
    send_attn(1)
    make_middle(1)
    mixer_sum(1, mbuf.at[0])
    pass_on("hfp", outq.at[1], hf.at[own])
    save0 = pltpu.make_async_copy(outq.at[1], out_ref.at[0], load_sem.at[10])
    save0.start()
    heads_pass("mid1", mid_rows(1))
    pass_got("hfp", lambda rows: hf.at[rows])
    pass_wait("hfp")
    choose(1, hf)
    mixer_in(2, mbuf.at[1])
    mixer_out(2)
    mixer_pass(2)
    mixer_sum(2, mbuf.at[1])
    save1 = pltpu.make_async_copy(outq.at[2], out_ref.at[1], load_sem.at[11])
    save1.start()
    assert len(index) <= SENDS, len(index)
    for key in pool.values():
        only(sends[key], descs[key].wait_send)
    save0.wait()
    save1.wait()


def on_device(
    entering_hidden, entering_embed, incoming_embed, mixer_input_weight,
    input_output_matrix_weight, step_size_weight, mixer_output_weight, log_decay_rate,
    step_size_bias, skip_weight, shared_query_key_value, shared_output_weight, adapter_down,
    adapter_upward, calls,
):
    flip = lambda v: jnp.swapaxes(v, 1, 2)[0]
    hbm = pl.BlockSpec(memory_space=pl.ANY)
    vmem = pl.BlockSpec(memory_space=pltpu.VMEM)
    smem = pl.BlockSpec(memory_space=pltpu.SMEM)
    scratch = [
        ((4, 4, D, SEQ), BF),
        ((2, 16, 256, 224), BF),
        ((8, 2, 288, 640), BF),
        ((8, 2, 224, 128), BF),
        ((224, 64), BF),
        ((224, 128), BF),
        ((D, 896), BF),
        ((D, 128), BF),
        ((896, D), BF),
        ((2 * D, 128), BF),
        ((3, 128, 896), BF),
        ((3, 56, 896), BF),
        ((4, 896, 256), BF),
        ((4, 64, 768), BF),
        ((4, 64, 768), BF),
        ((4, 128, 768), BF),
        ((4, 128, 768), BF),
        ((64, 768), BF),
        ((4, 2, 128, 128), BF),
        ((4, 2, 8, 128), F32),
        ((2, 256, 768), F32),
        ((512, 896), BF),
        ((32, 896), BF),
        ((2, 896, 256), BF),
        ((2, 4, 128, 256), BF),
        ((2, 2, 128, 256), BF),
        ((2, 2, 128, 256), BF),
        ((2, 2, 128, 128), BF),
        ((2, 4, 128, 128), BF),
        ((2, D, SEQ), BF),
        ((D, SEQ), BF),
        ((2, D, SEQ), BF),
        ((SEQ, D), BF),
        ((SEQ, 896), BF),
        ((SEQ, 896), F32),
        ((D, SEQ), F32),
        ((128, 128), F32),
        ((3, 2, Q, SEQ), BF),
        ((3, 2, Q, SEQ), BF),
        ((3, 2, Q, SEQ), BF),
        ((3, Q, SEQ), BF),
    ]
    out = pl.pallas_call(
        kernel,
        out_shape=jax.ShapeDtypeStruct((2, Q, SEQ), BF),
        in_specs=[
            hbm, hbm, hbm, hbm, hbm, vmem, hbm, vmem, vmem, smem, hbm, vmem, hbm, hbm, smem,
        ],
        out_specs=hbm,
        scratch_shapes=[pltpu.VMEM(shape, dtype) for shape, dtype in scratch]
        + [
            pltpu.SemaphoreType.DMA((POOL,)),
            pltpu.SemaphoreType.DMA((SENDS,)),
            pltpu.SemaphoreType.DMA((12,)),
        ],
        compiler_params=pltpu.CompilerParams(
            collective_id=0, has_side_effects=True, vmem_limit_bytes=58 * 1024 * 1024
        ),
    )(
        flip(entering_hidden), flip(entering_embed), flip(incoming_embed), mixer_input_weight[0],
        input_output_matrix_weight[0], flip(step_size_weight), mixer_output_weight[0],
        log_decay_rate, step_size_bias, skip_weight,
        jnp.swapaxes(shared_query_key_value, 0, 1), shared_output_weight, adapter_down[0],
        jnp.swapaxes(adapter_upward[0], 0, 1), calls,
    )
    return jnp.swapaxes(out, 1, 2)[:, None]


def solution(mesh):
    in_specs = (
        P("section", None, "head"),
        P("section", None, "head"),
        P(None, None, "head"),
        P("section", None, "head"),
        P("section", None, None),
        P("section", None, "head"),
        P("section", "head", None),
        P("section", "head"),
        P("section", "head"),
        P("section", "head"),
        P("section", None, "head"),
        P("section", "head"),
        P("section", None, None),
        P("section", None, None, "head"),
        P("section"),
    )
    out_specs = P(None, "section", None, "head")
    return jax.shard_map(
        on_device, mesh=mesh, in_specs=in_specs, out_specs=out_specs, check_vma=False
    )
```

```python
import jax
import jax.numpy as jnp
from jax import lax
from jax.experimental import pallas as pl
from jax.experimental.pallas import tpu as pltpu
from jax.sharding import PartitionSpec as P

MESH = pl.DeviceIdType.MESH
BF = jnp.bfloat16
F32 = jnp.float32
NT = (((1,), (1,)), ((), ()))
TN = (((0,), (0,)), ((), ()))
HIGH = lax.Precision.HIGHEST
D = 1792
Q = 448
SEQ = 128
HEADS = 14
HEAD_WIDTH = 224
EPS = 1e-05
SENDS = 133
POOL = 48


def iota(shape, dim):
    return lax.broadcasted_iota(jnp.int32, shape, dim)


def dot(a, b, dims=(((1,), (0,)), ((), ()))):
    return lax.dot_general(a, b, dims, preferred_element_type=F32)


def silu(v):
    return v / (1.0 + jnp.exp(-v))


def softplus(v):
    return jnp.maximum(v, 0.0) + jnp.log(1.0 + jnp.exp(-jnp.abs(v)))


def kernel(
    h0_in, e0_in, inc_in, wmix_in, wio_in, wdt_ref, wom_in, decay_ref, bias_ref, skip_ref,
    qkv_in, wo_ref, down_in, up_in, calls_ref,
    out_ref,
    xall, xs, wg, wr, rep, lane, wmix, wom, wom4, down, up, qw, a2s, a2r, ups, upr, low, misc,
    acc, wog, wo32, mx, rs2s, rs2r, atb, atr, mid, hf, mbuf, ubuf, ybuf, xbuf, pbuf, sbuf, cbuf, rss,
    rsp, rsm,
    outq, send_sem, recv_sem, load_sem,
):
    s = lax.axis_index("section")
    h = lax.axis_index("head")
    x = lax.rem(s, 4)
    y = lax.rem(s // 4, 2)
    z = s // 8
    core = lax.rem(h, 2)
    base = s - x
    sec_up = lax.rem(z + 1, 8) * 8 + lax.rem(s, 8)
    sec_down = lax.rem(z + 7, 8) * 8 + lax.rem(s, 8)
    sec_y = s + 4 - 8 * y
    sec_next = lax.rem(s + 1, 64)
    sec_prev = lax.rem(s + 63, 64)
    x_next = lax.rem(x + 1, 4)
    x_prev = lax.rem(x + 3, 4)
    x_far = lax.rem(x + 2, 4)
    twin = h + 1 - 2 * core
    mate = lax.rem(h + 2, 4)
    far = lax.rem(twin + 2, 4)

    def line(j):
        return lax.rem(x + j, 4)

    index = {}
    descs = {}
    sends = {}

    def only(cond, act):
        if cond is None:
            act()
        else:
            pl.when(cond)(lambda: act())

    pool = {}

    def remote(key, src, dst, section, head):
        at = index.setdefault(key, len(index))
        slot = at % POOL
        before = pool.get(slot)
        if before != key:
            if before is not None:
                only(sends[before], descs[before].wait_send)
            pool[slot] = key
        return pltpu.make_async_remote_copy(
            src_ref=src, dst_ref=dst, send_sem=send_sem.at[slot], recv_sem=recv_sem.at[at],
            device_id={"section": section, "head": head}, device_id_type=MESH,
        )

    def start(key, src, dst, section=None, head=None, cond=None):
        descs[key] = remote(key, src, dst, s if section is None else section, h if head is None else head)
        sends[key] = cond
        only(cond, descs[key].start)

    def pass_on(name, src, dst):
        for key, head in (((name, "mate"), mate), ((name, "same"), h)):
            fresh = remote(key, inc_in, dst, sec_next, head)
            descs[key] = remote(key, src, dst, sec_next, head)
            sends[key] = None
            pl.when(s == 63)(fresh.start)
            pl.when(s != 63)(descs[key].start)

    def pass_got(name, buf_at):
        got(name, "same")
        got(name, "mate")
        for key, rows in (((name, "own"), own), ((name, "other"), rows_of(mate))):
            ref = buf_at(rows)
            start(key, ref, ref, None, twin)

    def pass_wait(name):
        got(name, "own")
        got(name, "other")

    def got(*key, cond=None):
        only(cond, descs[key].wait_recv)

    loads = {}

    def load(name, src, dst):
        loads[name] = pltpu.make_async_copy(src, dst, load_sem.at[len(loads)])
        loads[name].start()

    def rows_of(head):
        return pl.ds(pl.multiple_of(head * Q, Q), Q)

    own = rows_of(h)
    load("qkv", qkv_in, qw)
    load("h0", h0_in, xall.at[x, 0, own])
    load("e0", e0_in, xall.at[x, 1, own])
    load("down", down_in, down)
    load("up", up_in, up)
    load("wmix", wmix_in, wmix.at[:, pl.ds(0, 896)])
    load("wio", wio_in, wmix.at[:, pl.ds(896, 128)])
    load("wom", wom_in, wom)

    barrier = pltpu.get_barrier_semaphore()
    peers = [(base + line(j), h) for j in (1, 2, 3)] + [(s, twin), (s, mate), (s, far)]
    peers += [(sec_up, h), (sec_down, h), (sec_y, h), (sec_next, h), (sec_prev, h)]
    peers += [(sec_next, mate), (sec_prev, mate)]
    for section, head in peers:
        pl.semaphore_signal(
            barrier, inc=1, device_id={"section": section, "head": head}, device_id_type=MESH
        )
    def head_columns(block, i):
        first_tile = 224 * i // 128 * 128
        window = block[:, first_tile : min(first_tile + 384, 896)]
        width = window.shape[1]
        shift = (width - (224 * i - first_tile)) % width
        return (pltpu.roll(window, shift, axis=1) if shift else window)[:, 0:256]

    wo32[...] = jnp.zeros_like(wo32)
    wo32[0:28, :] = wo_ref[...]
    def owner(k):
        return (k >= 56) * 1 + (k >= 112) * 1 + (k >= 168) * 1

    k, c = iota((224, 64), 0), iota((224, 64), 1)
    rep[...] = jnp.where(16 * owner(k) + ((k - 56 * owner(k)) & 15) == c, 1.0, 0.0).astype(BF)
    k, c = iota((224, 128), 0), iota((224, 128), 1)
    lane[...] = jnp.where((c >> 5) == ((k - 56 * owner(k)) >> 4), 1.0, 0.0).astype(BF)

    def tiles(query, keys, values):
        at = iota((query.shape[0], 128), 1)
        rest = values[:, 128:256]
        return [
            query[:, 0:128],
            keys[:, 0:128],
            values[:, 0:128],
            jnp.where(at < 96, query[:, 128:256], pltpu.roll(rest, 96, axis=1)),
            jnp.where(at < 96, keys[:, 128:256], pltpu.roll(rest, 64, axis=1)),
            jnp.where((at >= 64) & (at < 96), rest, 0.0),
        ]

    loads["qkv"].wait()
    blocks = [qw[k].astype(F32) for k in range(3)]
    nothing = jnp.zeros((8, 128), F32)
    for i in range(4):
        cut = tiles(*[head_columns(blocks[k], i) for k in range(3)])
        last = jnp.concatenate([cut[5][48:56], nothing], axis=0)
        folded = pltpu.roll(cut[5][0:16], 64, axis=1) + pltpu.roll(cut[5][16:32], 96, axis=1)
        folded = folded + cut[5][32:48] + pltpu.roll(last, 32, axis=1)
        for t in range(5):
            spare = folded[8 * t : 8 * t + 8] if t < 2 else nothing
            a2s[i, :, 128 * t : 128 * t + 128] = jnp.concatenate([cut[t], spare], axis=0).astype(BF)
    pl.semaphore_wait(barrier, len(peers))

    def heads_start(name, src, dst, cond=None):
        start((name, "mate"), src, dst, None, mate, cond)
        start((name, "twin"), src, dst, None, twin, cond)

    def heads_pass(name, buf_at, cond=None):
        got(name, "mate", cond=cond)
        ref = buf_at(rows_of(mate))
        start((name, "pass"), ref, ref, None, twin, cond)

    def heads_wait(name, cond=None):
        got(name, "twin", cond=cond)
        got(name, "pass", cond=cond)

    for j in (2, 1, 3):
        start(("a2a", j), a2s.at[line(j)], a2r.at[x], base + line(j))
    heads_start("h0", h0_in, xall.at[x, 0, own])
    heads_start("e0", e0_in, xall.at[x, 1, own])
    first = x == 0
    fresh = remote(("e1p",), inc_in, xall.at[0, 3, own], sec_next, h)
    descs[("e1p",)] = remote(("e1p",), e0_in, xall.at[0, 3, own], sec_next, h)
    sends[("e1p",)] = x == 3
    pl.when(s == 63)(fresh.start)
    pl.when((x == 3) & (s != 63))(descs[("e1p",)].start)
    a2r[x] = a2s[x]
    r, c = iota((224, 256), 0), iota((224, 256), 1)
    compact = jnp.where(((c - 8 * (c >> 6)) == r) & ((c & 63) < 56), 1.0, 0.0).astype(BF)
    for j in (1, 2, 3):
        got("a2a", j)
    packed = jnp.concatenate([a2r[c] for c in range(4)], axis=0)
    wg[z, y, 0:224, :] = dot(compact, packed).astype(BF)
    for c in range(4):
        rest = [a2r[c, 48:64, 128 * t : 128 * t + 128].astype(F32)[8:16] for t in (0, 1)]
        wg[z, y, 224:240, 128 * c : 128 * c + 128] = jnp.concatenate(rest, axis=0).astype(BF)
    wg[z, y, 224:240, 512:640] = jnp.zeros((16, 128), BF)
    wg[z, y, 240:272, :] = wo32[:, 0:640]
    wg[z, y, 272:288, 0:256] = wo32[0:16, 640:896]
    wg[z, y, 272:288, 256:512] = wo32[16:32, 640:896]
    wg[z, y, 272:288, 512:640] = jnp.zeros((16, 128), BF)

    spans = {"c0": (0, 128), "c1": (128, 160), "w0": (0, 128), "w1": (128, 112), "o": (240, 48)}

    def push(way, other, dz, span):
        first_row, rows = spans[span]
        zz, yy = lax.rem(z + dz + 8, 8), (1 - y) if other else y
        ref = wg.at[zz, yy, pl.ds(first_row, rows)]
        section = {"down": sec_down, "up": sec_up, "y": sec_y}[way]
        start((way, other, dz, span), ref, ref, section)

    def here(way, other, dz, span):
        got(way, other, dz, span)

    def pump(step):
        if step == 0:
            for span in ("c0", "c1"):
                push("down", 0, 0, span)
                push("up", 0, 0, span)
                push("y", 0, 0, span)
        for at, span in ((1, "c0"), (1.5, "c1")):
            if step == at:
                here("down", 0, 0, span)
                push("down", 0, 1, span)
                push("y", 0, 1, span)
                here("up", 0, 0, span)
                push("up", 0, -1, span)
        if step == 2:
            here("down", 0, 1, "c0")
            push("down", 0, 2, "c0")
            push("y", 0, 2, "w0")
            here("up", 0, -1, "c0")
            push("up", 0, -2, "c0")
        if step == 2.5:
            here("down", 0, 1, "c1")
            push("down", 0, 2, "c1")
            here("up", 0, -1, "c1")
            push("up", 0, -2, "c1")
            push("y", 0, -2, "w1")
            push("y", 0, 2, "w1")
            push("y", 0, -2, "w0")
            push("y", 0, -1, "w1")
            for dz in (2, -2, -1):
                push("y", 0, dz, "o")
            here("y", 0, 0, "c0")
            push("up", 1, 0, "w0")
        if step == 3:
            here("down", 0, 2, "c0")
            push("down", 0, 3, "w0")
            here("up", 0, -2, "c0")
            here("up", 0, -2, "c1")
            push("up", 0, -3, "w1")
            here("down", 0, 2, "c1")
            here("y", 0, 0, "c1")
        if step == 4:
            here("y", 0, 1, "c0")
            here("y", 0, 1, "c1")
            here("y", 0, 2, "w0")
            push("down", 1, 2, "w0")
        if step == 5:
            here("y", 0, -2, "w1")
            push("up", 1, -2, "w1")
        if step == 6:
            here("y", 0, 2, "w1")
            push("down", 1, 2, "w1")
        if step == 7:
            here("y", 0, -2, "w0")
            push("up", 1, -2, "w0")
        if step == 8:
            here("down", 1, 2, "w0")
            push("down", 1, 3, "w0")
            here("up", 1, -2, "w1")
            push("up", 1, -3, "w1")
            push("down", 0, 3, "o")
        if step == 9:
            here("y", 0, 2, "o")
            push("down", 1, 2, "o")
            here("y", 0, -2, "o")
            push("up", 1, -2, "o")
        if step == 10:
            here("down", 1, 2, "o")
            push("down", 1, 3, "o")
        if step == 11:
            here("y", 0, -1, "o")
            here("down", 0, 3, "o")
            here("up", 1, -2, "o")
            here("down", 1, 3, "o")

    def unpack(other, places):
        for dz in places:
            zz, yy = lax.rem(z + dz + 8, 8), (1 - y) if other else y
            at = pl.multiple_of(zz * 64 + yy * 32, 32)
            wog[pl.ds(at, 32), 0:640] = wg[zz, yy, 240:272, :]
            wog[pl.ds(at, 16), 640:896] = wg[zz, yy, 272:288, 0:256]
            wog[pl.ds(at + 16, 16), 640:896] = wg[zz, yy, 272:288, 256:512]

    def line_rows(first, count):
        return pl.ds(pl.multiple_of(core * 896 + first, Q), count)

    def line_start(n):
        ref = xall.at[x, n, line_rows(0, 896)]
        start(("line", n, "next"), ref, ref, base + x_next)
        start(("line", n, "prev"), ref, ref, base + x_prev)

    def line_pass(n):
        got("line", n, "next")
        ref = xall.at[x_prev, n, line_rows(0, 448)]
        start(("line2", n, "next"), ref, ref, base + x_next)
        got("line", n, "prev")
        ref = xall.at[x_next, n, line_rows(448, 448)]
        start(("line2", n, "prev"), ref, ref, base + x_prev)
        for at, key in ((x_prev, 1), (x_next, 2)):
            ref = xall.at[at, n, line_rows(0, 896)]
            start(("share", n, key), ref, ref, None, twin)

    def line_share(n):
        got("line2", n, "next")
        got("line2", n, "prev")
        ref = xall.at[x_far, n, line_rows(0, 896)]
        start(("share", n, 3), ref, ref, None, twin)

    def line_first():
        whole = xall.at[0, 3, line_rows(0, 896)]
        start(("le", "next"), whole, whole, base + 1, None, first)
        start(("le", "prev"), whole, whole, base + 3, None, first)

    def line_first_pass():
        whole = xall.at[0, 3, line_rows(0, 896)]
        for key, at, rows in (("next", 1, line_rows(0, 448)), ("prev", 3, line_rows(448, 448))):
            got("le", key, cond=x == at)
            part = xall.at[0, 3, rows]
            start(("le2", key), part, part, base + 2, None, x == at)
        start(("le", "side"), whole, whole, None, twin, (x == 1) | (x == 3))

    def line_first_share():
        whole = xall.at[0, 3, line_rows(0, 896)]
        for key in ("next", "prev"):
            got("le2", key, cond=x == 2)
        start(("le", "far"), whole, whole, None, twin, x == 2)

    def line_first_wait():
        got("le", "side", cond=(x == 1) | (x == 3))
        got("le", "far", cond=x == 2)

    def line_wait(n):
        for key in (1, 2, 3):
            got("share", n, key)

    def state(c, n):
        if n != 3:
            return c, n
        if isinstance(c, int):
            return (c - 1, 1) if c else (0, 3)
        return jnp.maximum(c - 1, 0), jnp.where(c == 0, 3, 1)

    def row_scale(n):
        total = jnp.zeros((1, SEQ), F32)
        for part in (0, 1):
            def add(t, total):
                block = xall[*state(x, 2 * n + part), pl.ds(pl.multiple_of(t * 128, 128), 128), :].astype(F32)
                return total + jnp.sum(block * block, axis=0, keepdims=True)
            total = lax.fori_loop(0, 14, add, total)
        return lax.rsqrt(total / (2 * D) + EPS)

    def make_low(n):
        scale = row_scale(n)
        total = jnp.zeros((128, SEQ), F32)
        for part in (0, 1):
            total = total + dot(down[part * D : part * D + D, :], xall[*state(x, 2 * n + part)], TN)
        low[x, n] = (total * scale).astype(BF)
        rows = iota((8, 128), 0)
        mark = calls_ref[0].astype(F32)
        misc[x, n] = jnp.where(rows == 0, scale, mark)
        for j in (1, 2, 3):
            start(("low", n, j), low.at[x, n], low.at[x, n], base + line(j))
            start(("misc", n, j), misc.at[x, n], misc.at[x, n], base + line(j))

    def pack_up():
        blocks = [up[k].astype(F32) for k in range(3)]
        for i in range(4):
            cut = tiles(*[head_columns(blocks[k], i) for k in range(3)])
            for t in range(6):
                ups[i, :, 128 * t : 128 * t + 128] = cut[t].astype(BF)
        start(("up", "far"), ups.at[x_far], upr.at[x], base + x_far)
        start(("up", "next"), ups.at[x_next], upr.at[x], base + x_next)
        start(("up", "prev"), ups.at[x_prev], upr.at[x], base + x_prev)
        upr[x] = ups[x]

    def up_wait():
        for key in ("next", "prev", "far"):
            got("up", key)

    def wait_low(n):
        for j in (1, 2, 3):
            got("low", n, j)
            got("misc", n, j)

    def eye_column(row, size):
        r, c = iota((size, size), 0), iota((size, size), 1)
        return jnp.sum(jnp.where(r == c, row, 0.0), axis=1, keepdims=True)

    def mixer_weights():
        cbuf[...] = jnp.zeros_like(cbuf)
        for t in range(14):
            cbuf[0:HEADS, :] = wdt_ref[:, 128 * t : 128 * t + 128].astype(F32)
            wmix[128 * t : 128 * t + 128, 1024:1152] = cbuf[...].T.astype(BF)
            wmix[128 * t : 128 * t + 128, 1152:1280] = jnp.zeros((128, 128), BF)

    def mixer_quarters():
        def body(t, carry):
            rows = pl.ds(pl.multiple_of(t * 128, 128), 128)
            low_lanes = iota((128, 128), 1) < 64
            for q in (0, 2):
                wom4[q, rows, 0:448] = wom[rows, 448 * q : 448 * q + 448]
            for q in (1, 3):
                first_tile = (448 * q - 64) // 128
                turned = [
                    pltpu.roll(wom[rows, 128 * k : 128 * k + 128].astype(F32), 64, axis=1)
                    for k in range(first_tile, first_tile + 4)
                ]
                for k in range(3):
                    wom4[q, rows, 128 * k : 128 * k + 128] = jnp.where(low_lanes, turned[k], turned[k + 1]).astype(BF)
                wom4[q, rows, 384:512] = jnp.where(low_lanes, turned[3], 0.0).astype(BF)
            for q in (0, 2):
                wom4[q, rows, 448:512] = jnp.zeros((128, 64), BF)
            return carry
        lax.fori_loop(0, 7, body, 0)

    def quarter_in(q, block, slot):
        total = jnp.sum(block * block, axis=0, keepdims=True)
        for t in range(3):
            ubuf[:, 128 * t : 128 * t + 128] = block[128 * t : 128 * t + 128].T.astype(BF)
        rest = jnp.concatenate([block[384:448], jnp.zeros((64, SEQ), F32)], axis=0)
        ubuf[:, 384:512] = rest.T.astype(BF)
        rows = rows_of(q)

        for t in range(5):
            xbuf[slot, :, 256 * t : 256 * t + 256] = dot(ubuf[:, 0:448], wmix[rows, 256 * t : 256 * t + 256])
        sbuf[slot : slot + 1, :] = total

    def mixed_columns(first_column):
        at = slice(first_column, first_column + 128)
        return (xbuf[0, :, at] + xbuf[1, :, at]) + (xbuf[2, :, at] + xbuf[3, :, at])

    def mixer_out(n, between=None):
        scale = eye_column(lax.rsqrt(jnp.sum(sbuf[0:4, :], axis=0, keepdims=True) / D + EPS), 128)
        bc = silu(mixed_columns(896) * scale)
        bias = eye_column(bias_ref[...], HEADS)
        rate = jnp.exp(eye_column(decay_ref[...], HEADS))
        dt = softplus((mixed_columns(1024) * scale).T[0:HEADS] + bias)
        upper = jnp.where(iota((128, 128), 0) <= iota((128, 128), 1), 1.0, 0.0)
        cum = lax.dot_general(
            dt * rate, upper, (((1,), (0,)), ((), ())), precision=HIGH, preferred_element_type=F32
        )
        cbuf[...] = jnp.zeros_like(cbuf)
        cbuf[0:HEADS, :] = cum
        cum_t = cbuf[...].T
        lanes = iota((128, 128), 1)
        rolled = pltpu.roll(bc, 64, axis=1)
        inner = lax.dot_general(
            jnp.where(lanes < 64, rolled, 0.0), jnp.where(lanes < 64, bc, 0.0), NT,
            precision=HIGH, preferred_element_type=F32,
        )
        causal = iota((128, 128), 0) >= lanes
        for pair in range(HEADS // 2):
            mixes = []
            for j in (2 * pair, 2 * pair + 1):
                gap = jnp.where(causal, cum[j : j + 1, :] - cum_t[:, j : j + 1], -1e30)
                mixes.append((inner * jnp.exp(gap) * dt[j : j + 1, :]).astype(BF))
            block = silu(mixed_columns(128 * pair) * scale)
            both = dot(jnp.concatenate(mixes, axis=0), block.astype(BF))
            skip = jnp.where(lanes < 64, skip_ref[0, 2 * pair], skip_ref[0, 2 * pair + 1])
            mixed = jnp.where(lanes < 64, both[0:128], both[128:256]) + skip * block
            ybuf[:, 128 * pair : 128 * pair + 128] = mixed.astype(BF)

        def quarter(q):
            def columns(t, carry):
                at = pl.multiple_of(t * 256, 256)
                part = dot(ybuf[...], wom4[q, :, pl.ds(at, 256)])
                pbuf[q, pl.ds(at, 128), :] = part[:, 0:128].T
                pbuf[q, pl.ds(at + 128, 128), :] = part[:, 128:256].T
                return carry
            lax.fori_loop(0, 2, columns, 0)

        quarter(far)
        rss[n, 1] = pbuf[far, 0:Q, :].astype(BF)
        start(("rs", n, "far"), rss.at[n, 1], rsp.at[n, 1], None, twin)
        quarter(mate)
        got("rs", n, "far")
        rsm[n, 0] = (pbuf[mate, 0:Q, :] + rsp[n, 1].astype(F32)).astype(BF)
        start(("rs", n, "mate"), rsm.at[n, 0], rsm.at[n, 1], None, mate)
        if between is not None:
            between()
        quarter(twin)
        rss[n, 0] = pbuf[twin, 0:Q, :].astype(BF)
        start(("rs", n, "twin"), rss.at[n, 0], rsp.at[n, 0], None, twin)
        quarter(h)

    def mixer_sum(n, src):
        got("rs", n, "twin")
        total = src[own, :].astype(F32) + pbuf[h, 0:Q, :] + rsp[n, 0].astype(F32)
        got("rs", n, "mate")
        outq[n] = (total + rsm[n, 1].astype(F32)).astype(BF)

    def marks():
        return [misc[c, 0, 1:2, :] for c in range(3)]

    def marks_bf():
        return [m.astype(BF) for m in marks()]

    identity = jnp.where(iota((128, 128), 0) == iota((128, 128), 1), 1.0, 0.0).astype(BF)

    def pick(values, masks):
        return values[0] * masks[0] + values[1] * masks[1] + values[2] * masks[2]

    def spread(n, parts=(0, 1)):
        for part in parts:
            places = [state(c, 2 * n + part) for c in range(4)]

            def body(t, carry, part=part, places=places):
                at = pl.ds(pl.multiple_of(t * 224, 224), 224)
                chosen = pick([xall[*places[c], at, :] for c in range(3)], marks_bf())
                xs[n, 8 * part + t, 0:128, :] = dot(identity, chosen, NT).astype(BF)
                xs[n, 8 * part + t, 128:256, :] = dot(identity, xall[*places[3], at, :], NT).astype(BF)
                return carry
            lax.fori_loop(0, 8, body, 0)

    def project(n, other, dz):
        zz, yy = lax.rem(z + dz + 8, 8), (1 - y) if other else y
        rest = jnp.concatenate([wg[zz, yy, 224:240, 128 * g : 128 * g + 128] for g in range(4)], axis=0)
        wr[zz, yy] = (dot(rep[...], rest) * lane[...].astype(F32)).astype(BF)
        project_piece(n, zz, yy)

    def project_piece(n, zz, yy):
        rows = xs[n, 2 * zz + yy]
        acc[n, :, 0:640] += dot(rows, wg[zz, yy, 0:224, :])
        acc[n, :, 640:768] += dot(rows, wr[zz, yy])

    def attend(n):
        up_first = pick([upr[c] for c in range(3)], [m[:, 0:1] for m in marks_bf()])
        low_first = pick([low[c, n] for c in range(3)], marks_bf())
        scale_first = pick([misc[c, n, 0:1, :] for c in range(3)], marks())
        causal = iota((128, 128), 0) >= iota((128, 128), 1)
        for slot in (0, 1):
            low_t = low_first if slot == 0 else low[3, n]
            up_slot = up_first if slot == 0 else upr[3]
            scale = eye_column(scale_first if slot == 0 else misc[3, n, 0:1, :], 128)
            rows = slice(128 * slot, 128 * slot + 128)
            total = acc[n, rows, :] * scale
            rest = total[:, 640:768]
            rest = rest + pltpu.roll(rest, 64, axis=1)
            rest = rest + pltpu.roll(rest, 32, axis=1)
            delta = dot(low_t, up_slot, TN)
            proj = [total[:, 128 * t : 128 * t + 128] + delta[:, 128 * t : 128 * t + 128] for t in range(5)]
            proj.append(rest + delta[:, 640:768])
            at = iota((128, 128), 1)
            tail = jnp.where(
                at < 32,
                pltpu.roll(proj[3], 32, axis=1),
                jnp.where(at < 64, pltpu.roll(proj[4], 64, axis=1), jnp.where(at < 96, proj[5], 0.0)),
            )
            query = jnp.concatenate([proj[0], jnp.where(at < 96, proj[3], 0.0)], axis=1).astype(BF)
            keys = jnp.concatenate([proj[1], jnp.where(at < 96, proj[4], 0.0)], axis=1).astype(BF)
            values = jnp.concatenate([proj[2], tail], axis=1).astype(BF)
            scores = dot(query, keys, NT) * HEAD_WIDTH ** (-0.5)
            scores = jnp.where(causal, scores, -1e30)
            expd = jnp.exp(scores - jnp.max(scores, axis=-1, keepdims=True))
            probs = (expd / jnp.sum(expd, axis=-1, keepdims=True)).astype(BF)
            mixed = dot(probs, values)
            at = pl.multiple_of(224 * x, 32)
            mx[n, pl.ds(at, 128), rows] = mixed[:, 0:128].T.astype(BF)
            mx[n, pl.ds(at + 128, 96), rows] = mixed[:, 128:256].T[0:96].astype(BF)

    def send_mixed(n):
        block = mx.at[n, pl.ds(pl.multiple_of(224 * x, 32), 224)]
        start(("mx", n, "far"), block, block, base + x_far)
        start(("mx", n, "prev"), block, block, base + x_prev)
        start(("mx", n, "next"), block, block, base + x_next)

    pt = {}

    def out_project(n):
        for key in ("prev", "next", "far"):
            got("mx", n, key)
        for q in range(4):
            rows = slice(128 * q, 128 * q + 128)
            rs2s[n, q] = dot(wog[rows, :], mx[n]).astype(BF)
        for key, head in ((0, far), (1, mate), (2, twin)):
            start(("rs2", n, key), rs2s.at[n, head], rs2r.at[n, key], None, head)

    def send_attn(n):
        total = rs2s[n, h].astype(F32)
        for key in (2, 1, 0):
            got("rs2", n, key)
            total = total + rs2r[n, key].astype(F32)
        atb[n, 0] = total[:, 0:128].astype(BF)
        atb[n, 1] = total[:, 128:256].astype(BF)
        for j in (2, 1, 3):
            start(("at", n, j), atb.at[n, line(j) // 3], atr.at[n, x], base + line(j))
        atr[n, x] = atb[n, x // 3]

    def make_middle(n):
        for j in (1, 2, 3):
            got("at", n, j)
        r, c = iota((224, 256), 0), iota((224, 256), 1)
        home = (4 * ((c >> 5) & 1) + (c >> 6)) * 28 + (c & 31)
        order = jnp.where((r == home) & ((c & 31) < 28), 1.0, 0.0).astype(BF)
        for half in (0, 1):
            stack = jnp.concatenate([atr[n, i, 64 * half : 64 * half + 64, :] for i in range(4)], axis=0)
            at = pl.ds(pl.multiple_of(h * Q + 224 * half, 224), 224)
            mid[n, at, :] = (xall[x, 2 * n, at, :].astype(F32) + dot(order, stack)).astype(BF)
        heads_start("mid%d" % n, mid.at[n, own], mid.at[n, own])

    def mid_rows(n):
        return lambda rows: mid.at[n, rows]

    mark_here = calls_ref[0].astype(F32)

    def choose(n, q, plain, slot):
        rows = rows_of(q)
        called = mid[n, rows, :].astype(F32)
        block = (called * mark_here + plain[rows, :].astype(F32) * (1.0 - mark_here)).astype(BF)
        if slot == 0:
            mbuf[n, rows, :] = block
        quarter_in(q, block.astype(F32), slot)

    def project_rest(first_piece, end):
        def body(t, carry):
            zz = t // 2
            project_piece(1, zz, t - 2 * zz)
            return carry
        lax.fori_loop(first_piece, end, body, 0)

    def state_rows(n):
        return lambda rows: xall.at[x, n, rows]

    pump(0)
    loads["h0"].wait()
    loads["e0"].wait()
    heads_pass("h0", state_rows(0))
    heads_pass("e0", state_rows(1))
    heads_wait("h0")
    line_start(0)
    heads_wait("e0")
    line_start(1)
    got("e1p", cond=first)
    e1_rows = lambda rows: xall.at[0, 3, rows]
    heads_start("e1", e1_rows(own), e1_rows(own), first)
    loads["wmix"].wait()
    loads["wio"].wait()
    mixer_weights()
    for q in range(4):
        quarter_in(q, xall[x, 0, Q * q : Q * q + Q, :].astype(F32), q)
    loads["wom"].wait()
    mixer_quarters()
    pump(1)
    mixer_out(0)
    pump(1.5)
    line_pass(0)
    heads_pass("e1", e1_rows, first)
    loads["down"].wait()
    make_low(0)
    line_pass(1)
    pump(2)
    heads_wait("e1", first)
    line_first()
    line_share(0)
    pump(2.5)
    mixer_sum(0, xall.at[x, 0])
    pass_on("h1p", outq.at[0], xall.at[x_next, 2, own])
    line_share(1)
    loads["up"].wait()
    pack_up()
    acc[0] = jnp.zeros((256, 768), F32)
    acc[1] = jnp.zeros((256, 768), F32)
    wait_low(0)
    line_wait(0)
    line_wait(1)
    spread(0, (0,))
    pump(3)
    pump(4)
    line_first_pass()
    spread(0, (1,))
    pump(5)
    for dz in (0, 1, -1, 2, -2):
        project(0, 0, dz)
    pump(6)
    line_first_share()
    unpack(0, (0, 1, -1, 2, -2, 3, -3))
    unpack(1, (0, 1))
    pass_got("h1p", state_rows(2))
    line_first_wait()
    spread(1, (1,))
    pump(7)
    pump(8)
    project(0, 1, 0)
    project(0, 1, 1)
    pass_wait("h1p")
    line_start(2)
    make_low(1)
    here("down", 0, 3, "w0")
    here("up", 0, -3, "w1")
    project(0, 0, 3)
    project(0, 0, -3)
    project(0, 0, 4)
    here("down", 1, 2, "w1")
    here("up", 1, -2, "w0")
    for dz in (2, -2, 3, -3):
        project(0, 1, dz)
    here("y", 0, -1, "w1")
    here("up", 1, 0, "w0")
    project(0, 1, -1)
    here("down", 1, 3, "w0")
    here("up", 1, -3, "w1")
    project(0, 1, 4)
    up_wait()
    pump(9)
    attend(0)
    send_mixed(0)
    pump(10)
    line_pass(2)
    project_rest(8, 16)
    pump(11)
    unpack(0, (4,))
    unpack(1, (-1, 2, -2, 3, -3, 4))
    out_project(0)
    line_share(2)
    wait_low(1)
    line_wait(2)
    spread(1, (0,))
    send_attn(0)
    project_rest(0, 8)
    attend(1)
    send_mixed(1)
    make_middle(0)
    choose(0, h, xall.at[x, 0], 0)
    got("mid0", "twin")
    choose(0, twin, xall.at[x, 0], 1)
    heads_pass("mid0", mid_rows(0))
    out_project(1)
    choose(0, mate, xall.at[x, 0], 2)
    got("mid0", "pass")
    choose(0, far, xall.at[x, 0], 3)
    mixer_out(1, lambda: send_attn(1))
    make_middle(1)
    mixer_sum(1, mbuf.at[0])
    pass_on("hfp", outq.at[1], hf.at[own])
    save0 = pltpu.make_async_copy(outq.at[1], out_ref.at[0], load_sem.at[10])
    save0.start()
    heads_pass("mid1", mid_rows(1))
    pass_got("hfp", lambda rows: hf.at[rows])
    choose(1, h, hf, 0)
    choose(1, mate, hf, 1)
    heads_wait("mid1")
    pass_wait("hfp")
    choose(1, twin, hf, 2)
    choose(1, far, hf, 3)
    mixer_out(2)
    mixer_sum(2, mbuf.at[1])
    save1 = pltpu.make_async_copy(outq.at[2], out_ref.at[1], load_sem.at[11])
    save1.start()
    assert len(index) == SENDS, len(index)
    for key in pool.values():
        only(sends[key], descs[key].wait_send)
    save0.wait()
    save1.wait()


def on_device(
    entering_hidden, entering_embed, incoming_embed, mixer_input_weight,
    input_output_matrix_weight, step_size_weight, mixer_output_weight, log_decay_rate,
    step_size_bias, skip_weight, shared_query_key_value, shared_output_weight, adapter_down,
    adapter_upward, calls,
):
    flip = lambda v: jnp.swapaxes(v, 1, 2)[0]
    hbm = pl.BlockSpec(memory_space=pl.ANY)
    vmem = pl.BlockSpec(memory_space=pltpu.VMEM)
    smem = pl.BlockSpec(memory_space=pltpu.SMEM)
    scratch = [
        ((4, 4, D, SEQ), BF),
        ((2, 16, 256, 224), BF),
        ((8, 2, 288, 640), BF),
        ((8, 2, 224, 128), BF),
        ((224, 64), BF),
        ((224, 128), BF),
        ((D, 1280), BF),
        ((896, D), BF),
        ((4, 896, 512), BF),
        ((2 * D, 128), BF),
        ((3, 128, 896), BF),
        ((3, 56, 896), BF),
        ((4, 64, 640), BF),
        ((4, 64, 640), BF),
        ((4, 128, 768), BF),
        ((4, 128, 768), BF),
        ((4, 2, 128, 128), BF),
        ((4, 2, 8, 128), F32),
        ((2, 256, 768), F32),
        ((512, 896), BF),
        ((32, 896), BF),
        ((2, 896, 256), BF),
        ((2, 4, 128, 256), BF),
        ((2, 3, 128, 256), BF),
        ((2, 2, 128, 128), BF),
        ((2, 4, 128, 128), BF),
        ((2, D, SEQ), BF),
        ((D, SEQ), BF),
        ((2, D, SEQ), BF),
        ((SEQ, 512), BF),
        ((SEQ, 896), BF),
        ((4, SEQ, 1280), F32),
        ((4, 512, SEQ), F32),
        ((8, SEQ), F32),
        ((128, 128), F32),
        ((3, 2, Q, SEQ), BF),
        ((3, 2, Q, SEQ), BF),
        ((3, 2, Q, SEQ), BF),
        ((3, Q, SEQ), BF),
    ]
    out = pl.pallas_call(
        kernel,
        out_shape=jax.ShapeDtypeStruct((2, Q, SEQ), BF),
        in_specs=[
            hbm, hbm, hbm, hbm, hbm, vmem, hbm, vmem, vmem, smem, hbm, vmem, hbm, hbm, smem,
        ],
        out_specs=hbm,
        scratch_shapes=[pltpu.VMEM(shape, dtype) for shape, dtype in scratch]
        + [
            pltpu.SemaphoreType.DMA((POOL,)),
            pltpu.SemaphoreType.DMA((SENDS,)),
            pltpu.SemaphoreType.DMA((12,)),
        ],
        compiler_params=pltpu.CompilerParams(
            collective_id=0, has_side_effects=True, vmem_limit_bytes=58 * 1024 * 1024
        ),
    )(
        flip(entering_hidden), flip(entering_embed), flip(incoming_embed), mixer_input_weight[0],
        input_output_matrix_weight[0], flip(step_size_weight), mixer_output_weight[0],
        log_decay_rate, step_size_bias, skip_weight,
        jnp.swapaxes(shared_query_key_value, 0, 1), shared_output_weight, adapter_down[0],
        jnp.swapaxes(adapter_upward[0], 0, 1), calls,
    )
    return jnp.swapaxes(out, 1, 2)[:, None]


def solution(mesh):
    in_specs = (
        P("section", None, "head"),
        P("section", None, "head"),
        P(None, None, "head"),
        P("section", None, "head"),
        P("section", None, None),
        P("section", None, "head"),
        P("section", "head", None),
        P("section", "head"),
        P("section", "head"),
        P("section", "head"),
        P("section", None, "head"),
        P("section", "head"),
        P("section", None, None),
        P("section", None, None, "head"),
        P("section"),
    )
    out_specs = P(None, "section", None, "head")
    return jax.shard_map(
        on_device, mesh=mesh, in_specs=in_specs, out_specs=out_specs, check_vma=False
    )
```

```python
import jax
import jax.numpy as jnp
from jax import lax
from jax.experimental import pallas as pl
from jax.experimental.pallas import tpu as pltpu
from jax.sharding import PartitionSpec as P

MESH = pl.DeviceIdType.MESH
BF = jnp.bfloat16
F32 = jnp.float32
NT = (((1,), (1,)), ((), ()))
TN = (((0,), (0,)), ((), ()))
HIGH = lax.Precision.HIGHEST
D = 1792
Q = 448
SEQ = 128
HEADS = 14
HEAD_WIDTH = 224
EPS = 1e-05
SENDS = 133
POOL = 48


def iota(shape, dim):
    return lax.broadcasted_iota(jnp.int32, shape, dim)


def dot(a, b, dims=(((1,), (0,)), ((), ()))):
    return lax.dot_general(a, b, dims, preferred_element_type=F32)


def silu(v):
    return v / (1.0 + jnp.exp(-v))


def softplus(v):
    return jnp.maximum(v, 0.0) + jnp.log(1.0 + jnp.exp(-jnp.abs(v)))


def kernel(
    h0_in, e0_in, inc_in, wmix_in, wio_in, wdt_ref, wom_in, decay_ref, bias_ref, skip_ref,
    qkv_in, wo_ref, down_in, up_in, calls_ref,
    out_ref,
    xall, xs, wg, wr, rep, lane, wmix, wom, wom4, down, up, qw, a2s, a2r, ups, upr, low, misc,
    acc, dbuf, cols, wog, wo32, mx, rs2s, rs2r, atb, atr, mid, hf, mbuf, ubuf, ybuf, xbuf, pbuf, sbuf, cbuf, rss,
    rsp, rsm,
    outq, send_sem, recv_sem, load_sem,
):
    s = lax.axis_index("section")
    h = lax.axis_index("head")
    x = lax.rem(s, 4)
    y = lax.rem(s // 4, 2)
    z = s // 8
    core = lax.rem(h, 2)
    base = s - x
    sec_up = lax.rem(z + 1, 8) * 8 + lax.rem(s, 8)
    sec_down = lax.rem(z + 7, 8) * 8 + lax.rem(s, 8)
    sec_y = s + 4 - 8 * y
    sec_next = lax.rem(s + 1, 64)
    sec_prev = lax.rem(s + 63, 64)
    x_next = lax.rem(x + 1, 4)
    x_prev = lax.rem(x + 3, 4)
    x_far = lax.rem(x + 2, 4)
    twin = h + 1 - 2 * core
    mate = lax.rem(h + 2, 4)
    far = lax.rem(twin + 2, 4)

    def line(j):
        return lax.rem(x + j, 4)

    index = {}
    descs = {}
    sends = {}

    def only(cond, act):
        if cond is None:
            act()
        else:
            pl.when(cond)(lambda: act())

    pool = {}

    def remote(key, src, dst, section, head):
        at = index.setdefault(key, len(index))
        slot = at % POOL
        before = pool.get(slot)
        if before != key:
            if before is not None:
                only(sends[before], descs[before].wait_send)
            pool[slot] = key
        return pltpu.make_async_remote_copy(
            src_ref=src, dst_ref=dst, send_sem=send_sem.at[slot], recv_sem=recv_sem.at[at],
            device_id={"section": section, "head": head}, device_id_type=MESH,
        )

    def start(key, src, dst, section=None, head=None, cond=None):
        descs[key] = remote(key, src, dst, s if section is None else section, h if head is None else head)
        sends[key] = cond
        only(cond, descs[key].start)

    def pass_on(name, src, dst):
        for key, head in (((name, "mate"), mate), ((name, "same"), h)):
            fresh = remote(key, inc_in, dst, sec_next, head)
            descs[key] = remote(key, src, dst, sec_next, head)
            sends[key] = None
            pl.when(s == 63)(fresh.start)
            pl.when(s != 63)(descs[key].start)

    def pass_got(name, buf_at):
        got(name, "same")
        got(name, "mate")
        for key, rows in (((name, "own"), own), ((name, "other"), rows_of(mate))):
            ref = buf_at(rows)
            start(key, ref, ref, None, twin)

    def pass_wait(name):
        got(name, "own")
        got(name, "other")

    def got(*key, cond=None):
        only(cond, descs[key].wait_recv)

    loads = {}

    def load(name, src, dst):
        loads[name] = pltpu.make_async_copy(src, dst, load_sem.at[len(loads)])
        loads[name].start()

    def rows_of(head):
        return pl.ds(pl.multiple_of(head * Q, Q), Q)

    own = rows_of(h)
    load("qkv", qkv_in, qw)
    load("h0", h0_in, xall.at[x, 0, own])
    load("e0", e0_in, xall.at[x, 1, own])
    load("down", down_in, down)
    load("up", up_in, up)
    load("wmix", wmix_in, wmix.at[:, pl.ds(0, 896)])
    load("wio", wio_in, wmix.at[:, pl.ds(896, 128)])
    load("wom", wom_in, wom)

    barrier = pltpu.get_barrier_semaphore()
    peers = [(base + line(j), h) for j in (1, 2, 3)] + [(s, twin), (s, mate), (s, far)]
    peers += [(sec_up, h), (sec_down, h), (sec_y, h), (sec_next, h), (sec_prev, h)]
    peers += [(sec_next, mate), (sec_prev, mate)]
    for section, head in peers:
        pl.semaphore_signal(
            barrier, inc=1, device_id={"section": section, "head": head}, device_id_type=MESH
        )
    def head_columns(block, i):
        first_tile = 224 * i // 128 * 128
        window = block[:, first_tile : min(first_tile + 384, 896)]
        width = window.shape[1]
        shift = (width - (224 * i - first_tile)) % width
        return (pltpu.roll(window, shift, axis=1) if shift else window)[:, 0:256]

    def tiles(query, keys, values):
        at = iota((query.shape[0], 128), 1)
        rest = values[:, 128:256]
        return [
            query[:, 0:128],
            keys[:, 0:128],
            values[:, 0:128],
            jnp.where(at < 96, query[:, 128:256], pltpu.roll(rest, 96, axis=1)),
            jnp.where(at < 96, keys[:, 128:256], pltpu.roll(rest, 64, axis=1)),
            jnp.where((at >= 64) & (at < 96), rest, 0.0),
        ]

    loads["qkv"].wait()
    blocks = [qw[k].astype(F32) for k in range(3)]
    nothing = jnp.zeros((8, 128), F32)
    for i in range(4):
        cut = tiles(*[head_columns(blocks[k], i) for k in range(3)])
        last = jnp.concatenate([cut[5][48:56], nothing], axis=0)
        folded = pltpu.roll(cut[5][0:16], 64, axis=1) + pltpu.roll(cut[5][16:32], 96, axis=1)
        folded = folded + cut[5][32:48] + pltpu.roll(last, 32, axis=1)
        for t in range(5):
            spare = folded[8 * t : 8 * t + 8] if t < 2 else nothing
            a2s[i, :, 128 * t : 128 * t + 128] = jnp.concatenate([cut[t], spare], axis=0).astype(BF)
    pl.semaphore_wait(barrier, len(peers))

    def heads_start(name, src, dst, cond=None):
        start((name, "mate"), src, dst, None, mate, cond)
        start((name, "twin"), src, dst, None, twin, cond)

    def heads_pass(name, buf_at, cond=None):
        got(name, "mate", cond=cond)
        ref = buf_at(rows_of(mate))
        start((name, "pass"), ref, ref, None, twin, cond)

    def heads_wait(name, cond=None):
        got(name, "twin", cond=cond)
        got(name, "pass", cond=cond)

    for j in (2, 1, 3):
        start(("a2a", j), a2s.at[line(j)], a2r.at[x], base + line(j))
    heads_start("h0", h0_in, xall.at[x, 0, own])
    heads_start("e0", e0_in, xall.at[x, 1, own])
    first = x == 0
    fresh = remote(("e1p",), inc_in, xall.at[0, 3, own], sec_next, h)
    descs[("e1p",)] = remote(("e1p",), e0_in, xall.at[0, 3, own], sec_next, h)
    sends[("e1p",)] = x == 3
    pl.when(s == 63)(fresh.start)
    pl.when((x == 3) & (s != 63))(descs[("e1p",)].start)
    wo32[...] = jnp.zeros_like(wo32)
    wo32[0:28, :] = wo_ref[...]
    def owner(k):
        return (k >= 56) * 1 + (k >= 112) * 1 + (k >= 168) * 1

    k, c = iota((224, 64), 0), iota((224, 64), 1)
    rep[...] = jnp.where(16 * owner(k) + ((k - 56 * owner(k)) & 15) == c, 1.0, 0.0).astype(BF)
    k, c = iota((224, 128), 0), iota((224, 128), 1)
    lane[...] = jnp.where((c >> 5) == ((k - 56 * owner(k)) >> 4), 1.0, 0.0).astype(BF)

    a2r[x] = a2s[x]
    r, c = iota((224, 256), 0), iota((224, 256), 1)
    compact = jnp.where(((c - 8 * (c >> 6)) == r) & ((c & 63) < 56), 1.0, 0.0).astype(BF)
    for j in (1, 2, 3):
        got("a2a", j)
    packed = jnp.concatenate([a2r[c] for c in range(4)], axis=0)
    wg[z, y, 0:224, :] = dot(compact, packed).astype(BF)
    for c in range(4):
        rest = [a2r[c, 48:64, 128 * t : 128 * t + 128].astype(F32)[8:16] for t in (0, 1)]
        wg[z, y, 224:240, 128 * c : 128 * c + 128] = jnp.concatenate(rest, axis=0).astype(BF)
    wg[z, y, 224:240, 512:640] = jnp.zeros((16, 128), BF)
    wg[z, y, 240:272, :] = wo32[:, 0:640]
    wg[z, y, 272:288, 0:256] = wo32[0:16, 640:896]
    wg[z, y, 272:288, 256:512] = wo32[16:32, 640:896]
    wg[z, y, 272:288, 512:640] = jnp.zeros((16, 128), BF)

    spans = {"c0": (0, 128), "c1": (128, 160), "w0": (0, 128), "w1": (128, 112), "o": (240, 48)}

    def push(way, other, dz, span):
        first_row, rows = spans[span]
        zz, yy = lax.rem(z + dz + 8, 8), (1 - y) if other else y
        ref = wg.at[zz, yy, pl.ds(first_row, rows)]
        section = {"down": sec_down, "up": sec_up, "y": sec_y}[way]
        start((way, other, dz, span), ref, ref, section)

    def here(way, other, dz, span):
        got(way, other, dz, span)

    def pump(step):
        if step == 0:
            for span in ("c0", "c1"):
                push("down", 0, 0, span)
                push("up", 0, 0, span)
                push("y", 0, 0, span)
        for at, span in ((1, "c0"), (1.5, "c1")):
            if step == at:
                here("down", 0, 0, span)
                push("down", 0, 1, span)
                push("y", 0, 1, span)
                here("up", 0, 0, span)
                push("up", 0, -1, span)
        if step == 2:
            here("down", 0, 1, "c0")
            push("down", 0, 2, "c0")
            push("y", 0, 2, "w0")
            here("up", 0, -1, "c0")
            push("up", 0, -2, "c0")
        if step == 2.5:
            here("down", 0, 1, "c1")
            push("down", 0, 2, "c1")
            here("up", 0, -1, "c1")
            push("up", 0, -2, "c1")
            push("y", 0, -2, "w1")
            push("y", 0, 2, "w1")
            push("y", 0, -2, "w0")
            push("y", 0, -1, "w1")
            for dz in (2, -2, -1):
                push("y", 0, dz, "o")
            here("y", 0, 0, "c0")
            push("up", 1, 0, "w0")
        if step == 3:
            here("down", 0, 2, "c0")
            push("down", 0, 3, "w0")
            here("up", 0, -2, "c0")
            here("up", 0, -2, "c1")
            here("down", 0, 2, "c1")
            here("y", 0, 0, "c1")
        if step == 4:
            here("y", 0, 1, "c0")
            here("y", 0, 1, "c1")
            here("y", 0, 2, "w0")
            push("down", 1, 2, "w0")
        if step == 5:
            here("y", 0, -2, "w1")
            push("up", 1, -2, "w1")
            push("up", 0, -3, "w1")
        if step == 6:
            here("y", 0, 2, "w1")
            push("down", 1, 2, "w1")
        if step == 7:
            here("y", 0, -2, "w0")
            push("up", 1, -2, "w0")
        if step == 8:
            here("down", 1, 2, "w0")
            push("down", 1, 3, "w0")
            push("down", 0, 3, "o")
        if step == 6.5:
            here("up", 1, -2, "w1")
            push("up", 1, -3, "w1")
        if step == 9:
            here("y", 0, 2, "o")
            push("down", 1, 2, "o")
            here("y", 0, -2, "o")
            push("up", 1, -2, "o")
        if step == 10:
            here("down", 1, 2, "o")
            push("down", 1, 3, "o")
        if step == 11:
            here("y", 0, -1, "o")
            here("down", 0, 3, "o")
            here("up", 1, -2, "o")
            here("down", 1, 3, "o")

    def unpack(other, places):
        for dz in places:
            zz, yy = lax.rem(z + dz + 8, 8), (1 - y) if other else y
            at = pl.multiple_of(zz * 64 + yy * 32, 32)
            wog[pl.ds(at, 32), 0:640] = wg[zz, yy, 240:272, :]
            wog[pl.ds(at, 16), 640:896] = wg[zz, yy, 272:288, 0:256]
            wog[pl.ds(at + 16, 16), 640:896] = wg[zz, yy, 272:288, 256:512]

    def line_rows(first, count):
        return pl.ds(pl.multiple_of(core * 896 + first, Q), count)

    def line_start(n):
        ref = xall.at[x, n, line_rows(0, 896)]
        start(("line", n, "next"), ref, ref, base + x_next)
        start(("line", n, "prev"), ref, ref, base + x_prev)

    def line_pass(n):
        got("line", n, "next")
        ref = xall.at[x_prev, n, line_rows(0, 448)]
        start(("line2", n, "next"), ref, ref, base + x_next)
        got("line", n, "prev")
        ref = xall.at[x_next, n, line_rows(448, 448)]
        start(("line2", n, "prev"), ref, ref, base + x_prev)
        for at, key in ((x_prev, 1), (x_next, 2)):
            ref = xall.at[at, n, line_rows(0, 896)]
            start(("share", n, key), ref, ref, None, twin)

    def line_share(n):
        got("line2", n, "next")
        got("line2", n, "prev")
        ref = xall.at[x_far, n, line_rows(0, 896)]
        start(("share", n, 3), ref, ref, None, twin)

    def line_first():
        whole = xall.at[0, 3, line_rows(0, 896)]
        start(("le", "next"), whole, whole, base + 1, None, first)
        start(("le", "prev"), whole, whole, base + 3, None, first)

    def line_first_pass():
        whole = xall.at[0, 3, line_rows(0, 896)]
        for key, at, rows in (("next", 1, line_rows(0, 448)), ("prev", 3, line_rows(448, 448))):
            got("le", key, cond=x == at)
            part = xall.at[0, 3, rows]
            start(("le2", key), part, part, base + 2, None, x == at)
        start(("le", "side"), whole, whole, None, twin, (x == 1) | (x == 3))

    def line_first_share():
        whole = xall.at[0, 3, line_rows(0, 896)]
        for key in ("next", "prev"):
            got("le2", key, cond=x == 2)
        start(("le", "far"), whole, whole, None, twin, x == 2)

    def line_first_wait():
        got("le", "side", cond=(x == 1) | (x == 3))
        got("le", "far", cond=x == 2)

    def line_wait(n):
        for key in (1, 2, 3):
            got("share", n, key)

    def state(c, n):
        if n != 3:
            return c, n
        if isinstance(c, int):
            return (c - 1, 1) if c else (0, 3)
        return jnp.maximum(c - 1, 0), jnp.where(c == 0, 3, 1)

    def row_scale(n):
        total = jnp.zeros((1, SEQ), F32)
        for part in (0, 1):
            def add(t, total):
                block = xall[*state(x, 2 * n + part), pl.ds(pl.multiple_of(t * 128, 128), 128), :].astype(F32)
                return total + jnp.sum(block * block, axis=0, keepdims=True)
            total = lax.fori_loop(0, 14, add, total)
        return lax.rsqrt(total / (2 * D) + EPS)

    def make_low(n):
        scale = row_scale(n)
        total = jnp.zeros((128, SEQ), F32)
        for part in (0, 1):
            total = total + dot(down[part * D : part * D + D, :], xall[*state(x, 2 * n + part)], TN)
        low[x, n] = (total * scale).astype(BF)
        rows = iota((8, 128), 0)
        mark = calls_ref[0].astype(F32)
        misc[x, n] = jnp.where(rows == 0, scale, mark)
        for j in (1, 2, 3):
            start(("low", n, j), low.at[x, n], low.at[x, n], base + line(j))
            start(("misc", n, j), misc.at[x, n], misc.at[x, n], base + line(j))

    def pack_up():
        blocks = [up[k].astype(F32) for k in range(3)]
        for i in range(4):
            cut = tiles(*[head_columns(blocks[k], i) for k in range(3)])
            for t in range(6):
                ups[i, :, 128 * t : 128 * t + 128] = cut[t].astype(BF)
        start(("up", "far"), ups.at[x_far], upr.at[x], base + x_far)
        start(("up", "next"), ups.at[x_next], upr.at[x], base + x_next)
        start(("up", "prev"), ups.at[x_prev], upr.at[x], base + x_prev)
        upr[x] = ups[x]

    def up_wait():
        for key in ("next", "prev", "far"):
            got("up", key)

    def wait_low(n):
        for j in (1, 2, 3):
            got("low", n, j)
            got("misc", n, j)

    def eye_column(row, size):
        r, c = iota((size, size), 0), iota((size, size), 1)
        return jnp.sum(jnp.where(r == c, row, 0.0), axis=1, keepdims=True)

    def mixer_weights():
        cbuf[...] = jnp.zeros_like(cbuf)
        for t in range(14):
            cbuf[0:HEADS, :] = wdt_ref[:, 128 * t : 128 * t + 128].astype(F32)
            wmix[128 * t : 128 * t + 128, 1024:1152] = cbuf[...].T.astype(BF)
            wmix[128 * t : 128 * t + 128, 1152:1280] = jnp.zeros((128, 128), BF)

    def mixer_quarters():
        def body(t, carry):
            rows = pl.ds(pl.multiple_of(t * 128, 128), 128)
            low_lanes = iota((128, 128), 1) < 64
            for q in (0, 2):
                wom4[q, rows, 0:448] = wom[rows, 448 * q : 448 * q + 448]
            for q in (1, 3):
                first_tile = (448 * q - 64) // 128
                turned = [
                    pltpu.roll(wom[rows, 128 * k : 128 * k + 128].astype(F32), 64, axis=1)
                    for k in range(first_tile, first_tile + 4)
                ]
                for k in range(3):
                    wom4[q, rows, 128 * k : 128 * k + 128] = jnp.where(low_lanes, turned[k], turned[k + 1]).astype(BF)
                wom4[q, rows, 384:512] = jnp.where(low_lanes, turned[3], 0.0).astype(BF)
            for q in (0, 2):
                wom4[q, rows, 448:512] = jnp.zeros((128, 64), BF)
            return carry
        lax.fori_loop(0, 7, body, 0)

    def quarter_in(q, block, slot):
        total = jnp.sum(block * block, axis=0, keepdims=True)
        for t in range(3):
            ubuf[:, 128 * t : 128 * t + 128] = block[128 * t : 128 * t + 128].T.astype(BF)
        rest = jnp.concatenate([block[384:448], jnp.zeros((64, SEQ), F32)], axis=0)
        ubuf[:, 384:512] = rest.T.astype(BF)
        rows = rows_of(q)

        for t in range(5):
            xbuf[slot, :, 256 * t : 256 * t + 256] = dot(ubuf[:, 0:448], wmix[rows, 256 * t : 256 * t + 256])
        sbuf[slot : slot + 1, :] = total

    def mixed_columns(first_column):
        at = slice(first_column, first_column + 128)
        return (xbuf[0, :, at] + xbuf[1, :, at]) + (xbuf[2, :, at] + xbuf[3, :, at])

    def mixer_out(n, between=None):
        scale = eye_column(lax.rsqrt(jnp.sum(sbuf[0:4, :], axis=0, keepdims=True) / D + EPS), 128)
        bc = silu(mixed_columns(896) * scale)
        bias = eye_column(bias_ref[...], HEADS)
        rate = jnp.exp(eye_column(decay_ref[...], HEADS))
        dt = softplus((mixed_columns(1024) * scale).T[0:HEADS] + bias)
        upper = jnp.where(iota((128, 128), 0) <= iota((128, 128), 1), 1.0, 0.0)
        cum = lax.dot_general(
            dt * rate, upper, (((1,), (0,)), ((), ())), precision=HIGH, preferred_element_type=F32
        )
        cbuf[...] = jnp.zeros_like(cbuf)
        cbuf[0:HEADS, :] = cum
        cum_t = cbuf[...].T
        lanes = iota((128, 128), 1)
        rolled = pltpu.roll(bc, 64, axis=1)
        inner = lax.dot_general(
            jnp.where(lanes < 64, rolled, 0.0), jnp.where(lanes < 64, bc, 0.0), NT,
            precision=HIGH, preferred_element_type=F32,
        )
        causal = iota((128, 128), 0) >= lanes
        for pair in range(HEADS // 2):
            mixes = []
            for j in (2 * pair, 2 * pair + 1):
                gap = jnp.where(causal, cum[j : j + 1, :] - cum_t[:, j : j + 1], -1e30)
                mixes.append((inner * jnp.exp(gap) * dt[j : j + 1, :]).astype(BF))
            block = silu(mixed_columns(128 * pair) * scale)
            both = dot(jnp.concatenate(mixes, axis=0), block.astype(BF))
            skip = jnp.where(lanes < 64, skip_ref[0, 2 * pair], skip_ref[0, 2 * pair + 1])
            mixed = jnp.where(lanes < 64, both[0:128], both[128:256]) + skip * block
            ybuf[:, 128 * pair : 128 * pair + 128] = mixed.astype(BF)

        def quarter(q):
            def columns(t, carry):
                at = pl.multiple_of(t * 256, 256)
                part = dot(ybuf[...], wom4[q, :, pl.ds(at, 256)])
                pbuf[q, pl.ds(at, 128), :] = part[:, 0:128].T
                pbuf[q, pl.ds(at + 128, 128), :] = part[:, 128:256].T
                return carry
            lax.fori_loop(0, 2, columns, 0)

        quarter(far)
        rss[n, 1] = pbuf[far, 0:Q, :].astype(BF)
        start(("rs", n, "far"), rss.at[n, 1], rsp.at[n, 1], None, twin)
        quarter(mate)
        got("rs", n, "far")
        rsm[n, 0] = (pbuf[mate, 0:Q, :] + rsp[n, 1].astype(F32)).astype(BF)
        start(("rs", n, "mate"), rsm.at[n, 0], rsm.at[n, 1], None, mate)
        if between is not None:
            between()
        quarter(twin)
        rss[n, 0] = pbuf[twin, 0:Q, :].astype(BF)
        start(("rs", n, "twin"), rss.at[n, 0], rsp.at[n, 0], None, twin)
        quarter(h)

    def mixer_sum(n, src):
        got("rs", n, "twin")
        total = src[own, :].astype(F32) + pbuf[h, 0:Q, :] + rsp[n, 0].astype(F32)
        got("rs", n, "mate")
        outq[n] = (total + rsm[n, 1].astype(F32)).astype(BF)

    def marks():
        return [misc[c, 0, 1:2, :] for c in range(3)]

    def marks_bf():
        return [m.astype(BF) for m in marks()]

    identity = jnp.where(iota((128, 128), 0) == iota((128, 128), 1), 1.0, 0.0).astype(BF)

    def pick(values, masks):
        return values[0] * masks[0] + values[1] * masks[1] + values[2] * masks[2]

    def spread(n, parts=(0, 1)):
        for part in parts:
            places = [state(c, 2 * n + part) for c in range(4)]

            def body(t, carry, part=part, places=places):
                at = pl.ds(pl.multiple_of(t * 224, 224), 224)
                chosen = pick([xall[*places[c], at, :] for c in range(3)], marks_bf())
                xs[n, 8 * part + t, 0:128, :] = dot(identity, chosen, NT).astype(BF)
                xs[n, 8 * part + t, 128:256, :] = dot(identity, xall[*places[3], at, :], NT).astype(BF)
                return carry
            lax.fori_loop(0, 8, body, 0)

    def project(n, other, dz):
        zz, yy = lax.rem(z + dz + 8, 8), (1 - y) if other else y
        rest = jnp.concatenate([wg[zz, yy, 224:240, 128 * g : 128 * g + 128] for g in range(4)], axis=0)
        wr[zz, yy] = (dot(rep[...], rest) * lane[...].astype(F32)).astype(BF)
        project_piece(n, zz, yy)

    def project_piece(n, zz, yy):
        rows = xs[n, 2 * zz + yy]
        acc[n, :, 0:640] += dot(rows, wg[zz, yy, 0:224, :])
        acc[n, :, 640:768] += dot(rows, wr[zz, yy])

    def prepare(n):
        up_first = pick([upr[c] for c in range(3)], [m[:, 0:1] for m in marks_bf()])
        low_first = pick([low[c, n] for c in range(3)], marks_bf())
        scale_first = pick([misc[c, n, 0:1, :] for c in range(3)], marks())
        dbuf[n, 0:128, :] = dot(low_first, up_first, TN)
        dbuf[n, 128:256, :] = dot(low[3, n], upr[3], TN)
        cols[n, 0:128, :] = jnp.broadcast_to(eye_column(scale_first, 128), (128, 128))
        cols[n, 128:256, :] = jnp.broadcast_to(eye_column(misc[3, n, 0:1, :], 128), (128, 128))

    def attend(n):
        causal = iota((128, 128), 0) >= iota((128, 128), 1)
        for slot in (0, 1):
            rows = slice(128 * slot, 128 * slot + 128)
            scale = cols[n, rows, :]
            rest = acc[n, rows, 640:768] * scale
            rest = rest + pltpu.roll(rest, 64, axis=1)
            rest = rest + pltpu.roll(rest, 32, axis=1)
            delta = dbuf[n, rows, :]
            proj = [
                acc[n, rows, 128 * t : 128 * t + 128] * scale + delta[:, 128 * t : 128 * t + 128]
                for t in range(5)
            ]
            proj.append(rest + delta[:, 640:768])
            at = iota((128, 128), 1)
            tail = jnp.where(
                at < 32,
                pltpu.roll(proj[3], 32, axis=1),
                jnp.where(at < 64, pltpu.roll(proj[4], 64, axis=1), jnp.where(at < 96, proj[5], 0.0)),
            )
            query = jnp.concatenate([proj[0], jnp.where(at < 96, proj[3], 0.0)], axis=1).astype(BF)
            keys = jnp.concatenate([proj[1], jnp.where(at < 96, proj[4], 0.0)], axis=1).astype(BF)
            values = jnp.concatenate([proj[2], tail], axis=1).astype(BF)
            scores = dot(query, keys, NT) * HEAD_WIDTH ** (-0.5)
            scores = jnp.where(causal, scores, -1e30)
            expd = jnp.exp(scores - jnp.max(scores, axis=-1, keepdims=True))
            probs = (expd / jnp.sum(expd, axis=-1, keepdims=True)).astype(BF)
            mixed = dot(probs, values)
            at = pl.multiple_of(224 * x, 32)
            mx[n, pl.ds(at, 128), rows] = mixed[:, 0:128].T.astype(BF)
            mx[n, pl.ds(at + 128, 96), rows] = mixed[:, 128:256].T[0:96].astype(BF)

    def send_mixed(n):
        block = mx.at[n, pl.ds(pl.multiple_of(224 * x, 32), 224)]
        start(("mx", n, "far"), block, block, base + x_far)
        start(("mx", n, "prev"), block, block, base + x_prev)
        start(("mx", n, "next"), block, block, base + x_next)

    pt = {}

    def out_project(n):
        for key in ("prev", "next", "far"):
            got("mx", n, key)
        for q in range(4):
            rows = slice(128 * q, 128 * q + 128)
            rs2s[n, q] = dot(wog[rows, :], mx[n]).astype(BF)
        for key, head in ((0, far), (1, mate), (2, twin)):
            start(("rs2", n, key), rs2s.at[n, head], rs2r.at[n, key], None, head)

    def send_attn(n):
        total = rs2s[n, h].astype(F32)
        for key in (2, 1, 0):
            got("rs2", n, key)
            total = total + rs2r[n, key].astype(F32)
        atb[n, 0] = total[:, 0:128].astype(BF)
        atb[n, 1] = total[:, 128:256].astype(BF)
        for j in (2, 1, 3):
            start(("at", n, j), atb.at[n, line(j) // 3], atr.at[n, x], base + line(j))
        atr[n, x] = atb[n, x // 3]

    def make_middle(n):
        for j in (1, 2, 3):
            got("at", n, j)
        r, c = iota((224, 256), 0), iota((224, 256), 1)
        home = (4 * ((c >> 5) & 1) + (c >> 6)) * 28 + (c & 31)
        order = jnp.where((r == home) & ((c & 31) < 28), 1.0, 0.0).astype(BF)
        for half in (0, 1):
            stack = jnp.concatenate([atr[n, i, 64 * half : 64 * half + 64, :] for i in range(4)], axis=0)
            at = pl.ds(pl.multiple_of(h * Q + 224 * half, 224), 224)
            mid[n, at, :] = (xall[x, 2 * n, at, :].astype(F32) + dot(order, stack)).astype(BF)
        heads_start("mid%d" % n, mid.at[n, own], mid.at[n, own])

    def mid_rows(n):
        return lambda rows: mid.at[n, rows]

    mark_here = calls_ref[0].astype(F32)

    def choose(n, q, plain, slot):
        rows = rows_of(q)
        called = mid[n, rows, :].astype(F32)
        block = (called * mark_here + plain[rows, :].astype(F32) * (1.0 - mark_here)).astype(BF)
        if slot == 0:
            mbuf[n, rows, :] = block
        quarter_in(q, block.astype(F32), slot)

    def project_rest(first_piece, end):
        def body(t, carry):
            zz = t // 2
            project_piece(1, zz, t - 2 * zz)
            return carry
        lax.fori_loop(first_piece, end, body, 0)

    def state_rows(n):
        return lambda rows: xall.at[x, n, rows]

    pump(0)
    loads["h0"].wait()
    loads["e0"].wait()
    heads_pass("h0", state_rows(0))
    heads_pass("e0", state_rows(1))
    heads_wait("h0")
    line_start(0)
    heads_wait("e0")
    line_start(1)
    got("e1p", cond=first)
    e1_rows = lambda rows: xall.at[0, 3, rows]
    heads_start("e1", e1_rows(own), e1_rows(own), first)
    loads["wmix"].wait()
    loads["wio"].wait()
    mixer_weights()
    for q in range(4):
        quarter_in(q, xall[x, 0, Q * q : Q * q + Q, :].astype(F32), q)
    loads["wom"].wait()
    mixer_quarters()
    pump(1)
    mixer_out(0)
    pump(1.5)
    line_pass(0)
    heads_pass("e1", e1_rows, first)
    loads["down"].wait()
    make_low(0)
    line_pass(1)
    pump(2)
    heads_wait("e1", first)
    line_first()
    line_share(0)
    pump(2.5)
    mixer_sum(0, xall.at[x, 0])
    pass_on("h1p", outq.at[0], xall.at[x_next, 2, own])
    line_share(1)
    loads["up"].wait()
    pack_up()
    acc[0] = jnp.zeros((256, 768), F32)
    acc[1] = jnp.zeros((256, 768), F32)
    wait_low(0)
    line_wait(0)
    line_wait(1)
    spread(0, (0,))
    pump(3)
    pump(4)
    line_first_pass()
    pump(5)
    spread(0, (1,))
    for dz in (0, 1, -1, 2, -2):
        project(0, 0, dz)
    pump(6)
    line_first_share()
    pass_got("h1p", state_rows(2))
    pump(6.5)
    unpack(0, (0, 1, -1, 2, -2, 3, -3))
    unpack(1, (0, 1))
    project(0, 1, 0)
    project(0, 1, 1)
    pump(7)
    pump(8)
    line_first_wait()
    spread(1, (1,))
    pass_wait("h1p")
    line_start(2)
    project(0, 1, 2)
    project(0, 1, -2)
    make_low(1)
    up_wait()
    prepare(0)
    here("down", 0, 3, "w0")
    here("up", 0, -3, "w1")
    project(0, 0, 3)
    project(0, 0, -3)
    project(0, 0, 4)
    here("down", 1, 2, "w1")
    project(0, 1, 3)
    here("y", 0, -1, "w1")
    here("up", 1, 0, "w0")
    project(0, 1, -1)
    here("up", 1, -2, "w0")
    project(0, 1, -3)
    here("down", 1, 3, "w0")
    here("up", 1, -3, "w1")
    project(0, 1, 4)
    pump(9)
    attend(0)
    send_mixed(0)
    project_rest(8, 12)
    pump(10)
    line_pass(2)
    project_rest(12, 16)
    pump(11)
    unpack(0, (4,))
    unpack(1, (-1, 2, -2, 3, -3, 4))
    out_project(0)
    line_share(2)
    wait_low(1)
    line_wait(2)
    spread(1, (0,))
    send_attn(0)
    project_rest(0, 8)
    prepare(1)
    attend(1)
    send_mixed(1)
    make_middle(0)
    choose(0, h, xall.at[x, 0], 0)
    got("mid0", "twin")
    choose(0, twin, xall.at[x, 0], 1)
    heads_pass("mid0", mid_rows(0))
    out_project(1)
    choose(0, mate, xall.at[x, 0], 2)
    got("mid0", "pass")
    choose(0, far, xall.at[x, 0], 3)
    mixer_out(1, lambda: send_attn(1))
    make_middle(1)
    mixer_sum(1, mbuf.at[0])
    pass_on("hfp", outq.at[1], hf.at[own])
    save0 = pltpu.make_async_copy(outq.at[1], out_ref.at[0], load_sem.at[10])
    save0.start()
    heads_pass("mid1", mid_rows(1))
    pass_got("hfp", lambda rows: hf.at[rows])
    choose(1, h, hf, 0)
    choose(1, mate, hf, 1)
    heads_wait("mid1")
    pass_wait("hfp")
    choose(1, twin, hf, 2)
    choose(1, far, hf, 3)
    mixer_out(2)
    mixer_sum(2, mbuf.at[1])
    save1 = pltpu.make_async_copy(outq.at[2], out_ref.at[1], load_sem.at[11])
    save1.start()
    assert len(index) == SENDS, len(index)
    for key in pool.values():
        only(sends[key], descs[key].wait_send)
    save0.wait()
    save1.wait()


def on_device(
    entering_hidden, entering_embed, incoming_embed, mixer_input_weight,
    input_output_matrix_weight, step_size_weight, mixer_output_weight, log_decay_rate,
    step_size_bias, skip_weight, shared_query_key_value, shared_output_weight, adapter_down,
    adapter_upward, calls,
):
    flip = lambda v: jnp.swapaxes(v, 1, 2)[0]
    hbm = pl.BlockSpec(memory_space=pl.ANY)
    vmem = pl.BlockSpec(memory_space=pltpu.VMEM)
    smem = pl.BlockSpec(memory_space=pltpu.SMEM)
    scratch = [
        ((4, 4, D, SEQ), BF),
        ((2, 16, 256, 224), BF),
        ((8, 2, 288, 640), BF),
        ((8, 2, 224, 128), BF),
        ((224, 64), BF),
        ((224, 128), BF),
        ((D, 1280), BF),
        ((896, D), BF),
        ((4, 896, 512), BF),
        ((2 * D, 128), BF),
        ((3, 128, 896), BF),
        ((3, 56, 896), BF),
        ((4, 64, 640), BF),
        ((4, 64, 640), BF),
        ((4, 128, 768), BF),
        ((4, 128, 768), BF),
        ((4, 2, 128, 128), BF),
        ((4, 2, 8, 128), F32),
        ((2, 256, 768), F32),
        ((2, 256, 768), F32),
        ((2, 256, 128), F32),
        ((512, 896), BF),
        ((32, 896), BF),
        ((2, 896, 256), BF),
        ((2, 4, 128, 256), BF),
        ((2, 3, 128, 256), BF),
        ((2, 2, 128, 128), BF),
        ((2, 4, 128, 128), BF),
        ((2, D, SEQ), BF),
        ((D, SEQ), BF),
        ((2, D, SEQ), BF),
        ((SEQ, 512), BF),
        ((SEQ, 896), BF),
        ((4, SEQ, 1280), F32),
        ((4, 512, SEQ), F32),
        ((8, SEQ), F32),
        ((128, 128), F32),
        ((3, 2, Q, SEQ), BF),
        ((3, 2, Q, SEQ), BF),
        ((3, 2, Q, SEQ), BF),
        ((3, Q, SEQ), BF),
    ]
    out = pl.pallas_call(
        kernel,
        out_shape=jax.ShapeDtypeStruct((2, Q, SEQ), BF),
        in_specs=[
            hbm, hbm, hbm, hbm, hbm, vmem, hbm, vmem, vmem, smem, hbm, vmem, hbm, hbm, smem,
        ],
        out_specs=hbm,
        scratch_shapes=[pltpu.VMEM(shape, dtype) for shape, dtype in scratch]
        + [
            pltpu.SemaphoreType.DMA((POOL,)),
            pltpu.SemaphoreType.DMA((SENDS,)),
            pltpu.SemaphoreType.DMA((12,)),
        ],
        compiler_params=pltpu.CompilerParams(
            collective_id=0, has_side_effects=True, vmem_limit_bytes=58 * 1024 * 1024
        ),
    )(
        flip(entering_hidden), flip(entering_embed), flip(incoming_embed), mixer_input_weight[0],
        input_output_matrix_weight[0], flip(step_size_weight), mixer_output_weight[0],
        log_decay_rate, step_size_bias, skip_weight,
        jnp.swapaxes(shared_query_key_value, 0, 1), shared_output_weight, adapter_down[0],
        jnp.swapaxes(adapter_upward[0], 0, 1), calls,
    )
    return jnp.swapaxes(out, 1, 2)[:, None]


def solution(mesh):
    in_specs = (
        P("section", None, "head"),
        P("section", None, "head"),
        P(None, None, "head"),
        P("section", None, "head"),
        P("section", None, None),
        P("section", None, "head"),
        P("section", "head", None),
        P("section", "head"),
        P("section", "head"),
        P("section", "head"),
        P("section", None, "head"),
        P("section", "head"),
        P("section", None, None),
        P("section", None, None, "head"),
        P("section"),
    )
    out_specs = P(None, "section", None, "head")
    return jax.shard_map(
        on_device, mesh=mesh, in_specs=in_specs, out_specs=out_specs, check_vma=False
    )
```
